512 devices in a mesh: snap: 8 (over x, core), node: 64 (over y, z).
Axes of the slice: x: 4, y: 4, z: 16, core: 2. Of those that a mesh axis runs over, the one named last changes fastest.
Arguments:
- features: bfloat16 [8, 65536, 512], P('snap', 'node'), may hold values from -6 to 6
- tile_rows: int32 [8, 1792], P('snap', 'node'), may hold values from 0 to 511, as said below
- tile_cols: int32 [8, 1792], P('snap', 'node'), may hold values from 0 to 511, as said below
- tile_values: bfloat16 [8, 1792, 128, 128], P('snap', 'node'), may hold values from -0.125 to 0.125
- tile_count: int32 [8, 64], P('snap', 'node'), may hold values from 9 to 28, as said below
- w_graph: bfloat16 [512, 512], replicated, may hold values from -0.25 to 0.25
- norm_gain: float32 [512], replicated, may hold values from 0.5 to 1.5
- w_query: bfloat16 [512, 512], replicated
- w_key: bfloat16 [512, 512], replicated, may hold values from -0.25 to 0.25
- w_value: bfloat16 [512, 512], replicated, may hold values from -0.25 to 0.25
- w_out: bfloat16 [512, 512], replicated, may hold values from -0.25 to 0.25
Outputs:
- layer_out: bfloat16 [8, 65536, 512], P(None, ('node', 'snap'))
The draws below stay inside these ranges and needn't reach their ends.
Inputs may be any that keep to these rules, and one draw needn't show every extreme that they name: `tile_rows`: every slot held by node index j (slots j * 28 to (j + 1) * 28 - 1) names a row block of that index's own nodes. `tile_cols`: every slot held by node index j names a column block of the nodes held by node indices j - 2 to j + 2. Of each node index's slots, the first tile_count are live and the rest are ignored; in each snapshot some node index has all 28 live.
All inputs are finite; a program needn't handle non-finite values.
Results may differ from the reference program's by a relative error of at most 0.0086.
Values may be sent and summed in bfloat16 or wider, within the bound.
A program may use at most 64 MiB of HBM per device.

```python
import jax
import jax.numpy as jnp
from jax import lax

D = 512
HEADS = 8
HEAD_DIM = 64
TILE = 128
NODE_DEV = 1024
TILE_DEV = 28
SNAPS = 8
NODES = 65536
TILES = 1792


def draw_tile_rows(key, part):
    slots = jnp.arange(TILES)
    device = slots // TILE_DEV
    blocks_dev = NODE_DEV // TILE
    local = jax.random.randint(jax.random.fold_in(key, 11), (SNAPS, TILES), 0, blocks_dev)
    return (device[None, :] * blocks_dev + local).astype(jnp.int32)


def draw_tile_cols(key, part):
    key_a, key_b = jax.random.split(jax.random.fold_in(key, 23))
    slots = jnp.arange(TILES)
    device = slots // TILE_DEV
    within = slots % TILE_DEV
    blocks_dev = NODE_DEV // TILE
    devices = TILES // TILE_DEV
    offset = jax.random.randint(key_a, (SNAPS, TILES), -2, 3)
    offset = jnp.where(within[None, :] < 5, within[None, :] - 2, offset)
    target = jnp.clip(device[None, :] + offset, 0, devices - 1)
    local = jax.random.randint(key_b, (SNAPS, TILES), 0, blocks_dev)
    return (target * blocks_dev + local).astype(jnp.int32)


def draw_tile_count(key, part):
    key_a, key_b = jax.random.split(jax.random.fold_in(key, 37))
    devices = TILES // TILE_DEV
    low = max(5, TILE_DEV // 3)
    count = jax.random.randint(key_a, (SNAPS, devices), low, TILE_DEV + 1)
    full = jax.random.randint(key_b, (SNAPS, 1), 0, devices)
    count = jnp.where(jnp.arange(devices)[None, :] == full, TILE_DEV, count)
    return count.astype(jnp.int32)


def draw_w_query(key, part):
    key_a = jax.random.fold_in(jax.random.fold_in(key, 53), 0)
    base = jax.random.normal(key_a, (D, D), jnp.float32) * D ** (-0.5)
    return base.astype(jnp.bfloat16)


def shard_levels(key, extent, cuts, least, largest):
    gain = 1.0
    for position, shards_of in cuts:
        draws = jax.random.uniform(jax.random.fold_in(jax.random.fold_in(key, 6), position), (shards_of,), jnp.float32, least / len(cuts), largest / len(cuts))
        gain = gain * jnp.repeat(jnp.exp(draws), extent[position] // shards_of).reshape((-1,) + (1,) * (len(extent) - 1 - position))
    return gain


def normal_values(own_key, shape, scale, limit, shards=(), kind=jnp.bfloat16):
    values = jax.random.normal(own_key, shape, jnp.float32) * scale
    if len(shards) > 0:
        values = shard_levels(own_key, shape, shards, -0.22, 0.18) * values
    return jnp.clip(values, min=-limit, max=limit).astype(kind)


def setup_inputs(seed: int = 0) -> dict:
    streams_of = jax.random.split(jax.random.key(seed), 12)
    return {
        "features": normal_values(streams_of[0], (SNAPS, NODES, D), 1.0, 6.0, ((0, 8), (1, 64))),
        "tile_rows": draw_tile_rows(jax.random.fold_in(streams_of[11], 71), 0),
        "tile_cols": draw_tile_cols(jax.random.fold_in(streams_of[11], 71), 0),
        "tile_values": normal_values(streams_of[3], (SNAPS, TILES, TILE, TILE), (TILE_DEV * 64) ** -0.5, 0.125, ((0, 8), (1, 64))),
        "tile_count": draw_tile_count(jax.random.fold_in(streams_of[11], 71), 0),
        "w_graph": normal_values(streams_of[5], (D, D), D ** -0.5, 0.25),
        "norm_gain": jnp.clip(1.0 + 0.1 * jax.random.normal(streams_of[6], (D,), jnp.float32), 0.5, 1.5),
        "w_query": draw_w_query(jax.random.fold_in(streams_of[11], 71), 0),
        "w_key": normal_values(streams_of[8], (D, D), D ** -0.5, 0.25),
        "w_value": normal_values(streams_of[9], (D, D), D ** -0.5, 0.25),
        "w_out": normal_values(streams_of[10], (D, D), D ** -0.5, 0.25),
    }


def norm_rows(hidden, norm_gain):
    value = hidden.astype(jnp.float32)
    mean = lax.optimization_barrier(jnp.mean(value, axis=-1, keepdims=True))
    centred = value - mean
    variance = lax.optimization_barrier(jnp.mean(centred * centred, axis=-1, keepdims=True))
    return (centred * lax.rsqrt(variance + 1e-05) * norm_gain).astype(jnp.bfloat16)

def snapshot_graph(feats, rows, cols, values, count, w_graph):
    blocks_dev = NODE_DEV // TILE
    blocks = feats.reshape(NODES // TILE, TILE, D)
    slots = jnp.arange(TILE_DEV).astype(jnp.int32)

    def one_device(carry, item):
        row_ids, col_ids, tiles, live_count, device = item
        picked = blocks[col_ids].astype(jnp.float32)
        prod = jnp.einsum('tij,tjd->tid', tiles.astype(jnp.float32), picked)
        prod = jnp.where((slots < live_count)[:, None, None], prod, jnp.float32(0.0))
        local = (row_ids - device * blocks_dev).astype(jnp.int32)
        summed = jax.ops.segment_sum(prod, local, num_segments=blocks_dev)
        return (carry, summed)
    devices = jnp.arange(NODES // NODE_DEV).astype(jnp.int32)
    unused, sums = lax.scan(one_device, jnp.float32(0.0), (rows, cols, values, count, devices))
    aggregated = sums.reshape(NODES, D).astype(jnp.bfloat16)
    mixed = jnp.dot(aggregated, w_graph, preferred_element_type=jnp.float32)
    return (feats.astype(jnp.float32) + jax.nn.relu(mixed)).astype(jnp.bfloat16)

def reference(features, tile_rows, tile_cols, tile_values, tile_count, w_graph, norm_gain, w_query, w_key, w_value, w_out):
    devices = NODES // NODE_DEV
    rows = tile_rows.reshape(SNAPS, devices, TILE_DEV)
    cols = tile_cols.reshape(SNAPS, devices, TILE_DEV)
    values = tile_values.reshape(SNAPS, devices, TILE_DEV, TILE, TILE)

    def per_snapshot(item):
        feats, row_ids, col_ids, tiles, count = item
        return snapshot_graph(feats, row_ids, col_ids, tiles, count, w_graph)
    hidden = lax.map(per_snapshot, (features, rows, cols, values, tile_count))
    normed = norm_rows(hidden, norm_gain).reshape(SNAPS * NODES, D)
    query = jnp.dot(normed, w_query, preferred_element_type=jnp.float32).astype(jnp.bfloat16)
    key = jnp.dot(normed, w_key, preferred_element_type=jnp.float32).astype(jnp.bfloat16)
    value = jnp.dot(normed, w_value, preferred_element_type=jnp.float32).astype(jnp.bfloat16)
    query = query.reshape(SNAPS, NODES, HEADS, HEAD_DIM).astype(jnp.float32)
    key = key.reshape(SNAPS, NODES, HEADS, HEAD_DIM).astype(jnp.float32)
    value = value.reshape(SNAPS, NODES, HEADS, HEAD_DIM).astype(jnp.float32)
    scores = jnp.einsum('snhd,unhd->nhsu', query, key) * HEAD_DIM ** (-0.5)
    later = jnp.arange(SNAPS)[:, None] >= jnp.arange(SNAPS)[None, :]
    scores = jnp.where(later, scores, jnp.float32(-1e+30))
    weights = jax.nn.softmax(scores, axis=-1).astype(jnp.bfloat16)
    context = jnp.einsum('nhsu,unhd->snhd', weights.astype(jnp.float32), value)
    context = context.astype(jnp.bfloat16).reshape(SNAPS * NODES, D)
    projected = jnp.dot(context, w_out, preferred_element_type=jnp.float32)
    result = hidden.reshape(SNAPS * NODES, D).astype(jnp.float32) + projected
    return result.astype(jnp.bfloat16).reshape(SNAPS, NODES, D)
```

```python
import jax
import jax.numpy as jnp
from jax import lax
from jax.experimental import pallas as pl
from jax.experimental.pallas import tpu as pltpu
from jax.sharding import PartitionSpec as P

MESH = pl.DeviceIdType.MESH
HEADS = 8
HEAD_DIM = 64
LANES = 128
BF16 = jnp.bfloat16
F32 = jnp.float32


def layer_kernel(
    snaps,
    ring,
    rows_ref,
    cols_ref,
    count_ref,
    feat,
    tiles_hbm,
    wg_hbm,
    gain_hbm,
    wq_hbm,
    wk_hbm,
    wv_hbm,
    wo_hbm,
    out,
    win_a,
    win_b,
    win_c,
    win_d,
    tiles,
    part,
    aggregated,
    resident_agg,
    resident_feat,
    mixed,
    hidden,
    query,
    key,
    value,
    wg,
    gain,
    wqkv,
    wo,
    gather_heads,
    spread_heads,
    out_buf,
    prev_ref,
    last_ref,
    own_send,
    own_recv,
    relay_send,
    relay_recv,
    feat_send,
    feat_recv,
    agg_send,
    agg_recv,
    local_sem,
    out_sem,
):
    win = (win_a, win_b, win_c, win_d)
    blocks = feat.shape[0]
    tile = feat.shape[1]
    width = feat.shape[2]
    chunks = width // LANES
    slots = tiles.shape[0]
    s = lax.axis_index("snap")
    j = lax.axis_index("node")
    right = lax.rem(j + 1, ring)
    left = lax.rem(j + ring - 1, ring)
    node_peer = (right, left)
    near = (blocks, 3 * blocks)
    far = (0, 4 * blocks)

    def cols_of(c):
        return pl.ds(c * LANES, LANES)

    local = [pltpu.make_async_copy(tiles_hbm, tiles, local_sem.at[0])]
    for c in range(chunks):
        local.append(
            pltpu.make_async_copy(
                feat.at[:, :, cols_of(c)], win[c].at[pl.ds(2 * blocks, blocks)], local_sem.at[1 + c]
            )
        )
    base = 1 + chunks
    weights = [
        pltpu.make_async_copy(wg_hbm, wg, local_sem.at[base]),
        pltpu.make_async_copy(gain_hbm, gain, local_sem.at[base + 1]),
        pltpu.make_async_copy(wq_hbm, wqkv.at[0], local_sem.at[base + 2]),
        pltpu.make_async_copy(wk_hbm, wqkv.at[1], local_sem.at[base + 3]),
        pltpu.make_async_copy(wv_hbm, wqkv.at[2], local_sem.at[base + 4]),
        pltpu.make_async_copy(wo_hbm, wo, local_sem.at[base + 5]),
        pltpu.make_async_copy(feat.at[s], resident_feat.at[s], local_sem.at[base + 6]),
    ]

    def own(c, d):
        return pltpu.make_async_remote_copy(
            src_ref=feat.at[:, :, cols_of(c)],
            dst_ref=win[c].at[pl.ds(near[d], blocks)],
            send_sem=own_send.at[d, c],
            recv_sem=own_recv.at[d, c],
            device_id=(s, node_peer[d]),
            device_id_type=MESH,
        )

    def relay(c, d):
        return pltpu.make_async_remote_copy(
            src_ref=win[c].at[pl.ds(near[d], blocks)],
            dst_ref=win[c].at[pl.ds(far[d], blocks)],
            send_sem=relay_send.at[d, c],
            recv_sem=relay_recv.at[d, c],
            device_id=(s, node_peer[d]),
            device_id_type=MESH,
        )

    def feat_to(d):
        p = lax.rem(s + d, snaps)
        return pltpu.make_async_remote_copy(
            src_ref=feat.at[p],
            dst_ref=resident_feat.at[s],
            send_sem=feat_send.at[d - 1],
            recv_sem=feat_recv.at[d - 1],
            device_id=(p, j),
            device_id_type=MESH,
        )

    def agg_to(c, d):
        p = lax.rem(s + d, snaps)
        return pltpu.make_async_remote_copy(
            src_ref=aggregated.at[c, p],
            dst_ref=resident_agg.at[c, s],
            send_sem=agg_send.at[c, d - 1],
            recv_sem=agg_recv.at[c, d - 1],
            device_id=(p, j),
            device_id_type=MESH,
        )

    barrier = pltpu.get_barrier_semaphore()
    for d in range(2):
        pl.semaphore_signal(barrier, inc=1, device_id=(s, node_peer[d]), device_id_type=MESH)
    for d in range(1, snaps):
        pl.semaphore_signal(barrier, inc=1, device_id=(lax.rem(s + d, snaps), j), device_id_type=MESH)
    for copy in local:
        copy.start()
    pl.semaphore_wait(barrier, 1 + snaps)

    for c in range(2):
        for d in range(2):
            own(c, d).start()
    for copy in weights:
        copy.start()
    for d in range(1, snaps):
        feat_to(d).start()

    live_slots = count_ref[0, 0]

    def link(t, last):
        row = rows_ref[0, t] - j * blocks
        before = jnp.int32(0)
        for r in range(blocks):
            before = jnp.where(row == r, last[r], before)
        prev_ref[t] = before
        live = t < live_slots
        return tuple(jnp.where((row == r) & live, t + 1, last[r]) for r in range(blocks))

    last = lax.fori_loop(0, slots, link, (jnp.int32(0),) * blocks)
    for r in range(blocks):
        last_ref[r] = last[r]

    feature = lax.broadcasted_iota(jnp.int32, (width, LANES), 0) // HEAD_DIM
    lane = lax.broadcasted_iota(jnp.int32, (width, LANES), 1)
    for u in range(snaps):
        hit = lax.rem(lane, snaps * HEADS) == u * HEADS + feature
        gather_heads[u] = jnp.where(hit, HEAD_DIM**-0.5, 0.0).astype(BF16)
    feature = lax.broadcasted_iota(jnp.int32, (LANES, width), 1) // HEAD_DIM
    lane = lax.broadcasted_iota(jnp.int32, (LANES, width), 0)
    for u in range(snaps):
        spread_heads[u] = jnp.where(lane == u * HEADS + feature, 1.0, 0.0).astype(BF16)
    part[0] = jnp.zeros((tile, LANES), F32)

    def aggregate(c):
        def product(t, carry):
            column = jnp.clip(cols_ref[0, t] - (j - 2) * blocks, 0, 5 * blocks - 1)
            part[t + 1] = jnp.dot(tiles[t], win[c][column], preferred_element_type=F32)
            return carry

        def step(i, carry):
            for k in range(4):
                product(i * 4 + k, carry)
            return carry

        lax.fori_loop(0, slots // 4, step, 0)
        for t in range(slots // 4 * 4, slots):
            product(t, 0)

        def chain(t, carry):
            part[t + 1] = part[t + 1] + part[prev_ref[t]]
            return carry

        lax.fori_loop(0, slots, chain, 0)
        for r in range(blocks):
            aggregated[c, r] = part[last_ref[r]].astype(BF16)
        for d in range(1, snaps):
            agg_to(c, d).start()
        resident_agg[c, s] = aggregated[c, s]

    for copy in local:
        copy.wait()

    def pass_on(c):
        for d in range(2):
            own(c, d).wait_recv()
            relay(c, d).start()
            if c + 2 < chunks:
                own(c + 2, d).start()

    def arrived(c):
        for d in range(2):
            relay(c, d).wait_recv()

    pass_on(0)
    pass_on(1)
    for c in range(chunks):
        arrived(c)
        aggregate(c)
        if c + 2 < chunks:
            pass_on(c + 2)
        if c == chunks - 2:
            for copy in weights:
                copy.wait()
            for c2 in range(2):
                for d in range(1, snaps):
                    agg_to(c2, d).wait_recv()
            for u in range(snaps):
                pair = jnp.concatenate([resident_agg[0, u], resident_agg[1, u]], axis=1)
                mixed[u] = jnp.dot(pair, wg[pl.ds(0, 2 * LANES)], preferred_element_type=F32)

    for d in range(1, snaps):
        feat_to(d).wait_recv()
    for c2 in range(2, chunks):
        for d in range(1, snaps):
            agg_to(c2, d).wait_recv()

    lane = lax.broadcasted_iota(jnp.int32, (tile, LANES), 1)
    lane_snap = lax.rem(lane, snaps * HEADS) // HEADS
    period = snaps * HEADS
    for t in range(snaps):
        pair = jnp.concatenate([resident_agg[2, t], resident_agg[3, t]], axis=1)
        total = mixed[t] + jnp.dot(pair, wg[pl.ds(2 * LANES, 2 * LANES)], preferred_element_type=F32)
        hid = (resident_feat[t].astype(F32) + jnp.maximum(total, 0.0)).astype(BF16)
        hidden[t] = hid
        hid = hid.astype(F32)
        mean = jnp.mean(hid, axis=-1, keepdims=True)
        centred = hid - mean
        variance = jnp.mean(centred * centred, axis=-1, keepdims=True)
        normed = (centred * lax.rsqrt(variance + 1e-05) * gain[...]).astype(BF16)
        query[t] = jnp.dot(normed, wqkv[0], preferred_element_type=F32).astype(BF16)
        key[t] = jnp.dot(normed, wqkv[1], preferred_element_type=F32).astype(BF16)
        value[t] = jnp.dot(normed, wqkv[2], preferred_element_type=F32).astype(BF16)

    for t in range(snaps):
        q = query[t]
        scores = jnp.zeros((tile, LANES), F32)
        for u in range(t + 1):
            scores = scores + jnp.dot(q * key[u], gather_heads[u], preferred_element_type=F32)
        scores = jnp.where(lane_snap <= t, scores, -1e30)
        top = scores
        shift = HEADS
        while shift < period:
            top = jnp.maximum(top, pltpu.roll(top, shift, 1))
            shift *= 2
        e = jnp.exp(scores - top)
        total = e
        shift = HEADS
        while shift < period:
            total = total + pltpu.roll(total, shift, 1)
            shift *= 2
        w = (e / total).astype(BF16)
        context = jnp.zeros((tile, width), F32)
        for u in range(t + 1):
            wide = jnp.dot(w, spread_heads[u], preferred_element_type=F32)
            context = context + wide * value[u].astype(F32)
        projected = jnp.dot(context.astype(BF16), wo[...], preferred_element_type=F32)
        out_buf[t] = (hidden[t].astype(F32) + projected).astype(BF16)
        pltpu.make_async_copy(out_buf.at[t], out.at[t], out_sem.at[t]).start()

    for c in range(chunks):
        for d in range(2):
            own(c, d).wait_send()
            relay(c, d).wait_send()
        for d in range(1, snaps):
            agg_to(c, d).wait_send()
    for d in range(1, snaps):
        feat_to(d).wait_send()
    for t in range(snaps):
        pltpu.make_async_copy(out_buf.at[t], out.at[t], out_sem.at[t]).wait()


def local_layer(
    snaps,
    ring,
    features,
    tile_rows,
    tile_cols,
    tile_values,
    tile_count,
    w_graph,
    norm_gain,
    w_query,
    w_key,
    w_value,
    w_out,
):
    nodes_dev, width = features.shape[1:]
    slots, tile = tile_values.shape[1:3]
    blocks = nodes_dev // tile
    chunks = width // LANES
    smem = pl.BlockSpec(memory_space=pltpu.SMEM)
    anywhere = pl.BlockSpec(memory_space=pl.ANY)
    dma = pltpu.SemaphoreType.DMA

    def kernel(*refs):
        layer_kernel(snaps, ring, *refs)

    return pl.pallas_call(
        kernel,
        out_shape=jax.ShapeDtypeStruct((snaps, tile, width), BF16),
        in_specs=[smem] * 3 + [anywhere] * 8,
        out_specs=anywhere,
        scratch_shapes=[
            *[pltpu.VMEM((5 * blocks, tile, LANES), BF16)] * chunks,
            pltpu.VMEM((slots, tile, tile), BF16),
            pltpu.VMEM((slots + 1, tile, LANES), F32),
            pltpu.VMEM((chunks, blocks, tile, LANES), BF16),
            pltpu.VMEM((chunks, snaps, tile, LANES), BF16),
            pltpu.VMEM((snaps, tile, width), BF16),
            pltpu.VMEM((snaps, tile, width), F32),
            pltpu.VMEM((snaps, tile, width), BF16),
            pltpu.VMEM((snaps, tile, width), BF16),
            pltpu.VMEM((snaps, tile, width), BF16),
            pltpu.VMEM((snaps, tile, width), BF16),
            pltpu.VMEM((width, width), BF16),
            pltpu.VMEM((1, width), F32),
            pltpu.VMEM((3, width, width), BF16),
            pltpu.VMEM((width, width), BF16),
            pltpu.VMEM((snaps, width, LANES), BF16),
            pltpu.VMEM((snaps, LANES, width), BF16),
            pltpu.VMEM((snaps, tile, width), BF16),
            pltpu.SMEM((slots,), jnp.int32),
            pltpu.SMEM((blocks,), jnp.int32),
            dma((2, chunks)),
            dma((2, chunks)),
            dma((2, chunks)),
            dma((2, chunks)),
            dma((snaps - 1,)),
            dma((snaps - 1,)),
            dma((chunks, snaps - 1)),
            dma((chunks, snaps - 1)),
            dma((8 + chunks,)),
            dma((snaps,)),
        ],
        compiler_params=pltpu.CompilerParams(
            collective_id=0, has_side_effects=True, vmem_limit_bytes=48 * 2**20
        ),
        cost_estimate=pl.CostEstimate(
            flops=4 * 10**9, bytes_accessed=6 * 2**20, transcendentals=10**6
        ),
    )(
        tile_rows,
        tile_cols,
        tile_count,
        features.reshape(blocks, tile, width),
        tile_values[0],
        w_graph,
        norm_gain.reshape(1, width),
        w_query,
        w_key,
        w_value,
        w_out,
    )


def solution(mesh):
    snaps, ring = mesh.shape["snap"], mesh.shape["node"]

    def local(*args):
        return local_layer(snaps, ring, *args)

    in_specs = (
        P("snap", "node", None),
        P("snap", "node"),
        P("snap", "node"),
        P("snap", "node", None, None),
        P("snap", "node"),
        P(),
        P(),
        P(),
        P(),
        P(),
        P(),
    )
    return jax.shard_map(
        local, mesh=mesh, in_specs=in_specs, out_specs=P(None, ("node", "snap"), None), check_vma=False
    )
```

```python
import jax
import jax.numpy as jnp
from jax import lax
from jax.experimental import pallas as pl
from jax.experimental.pallas import tpu as pltpu
from jax.sharding import PartitionSpec as P

MESH = pl.DeviceIdType.MESH
HEADS = 8
HEAD_DIM = 64
LANES = 128
BF16 = jnp.bfloat16
F32 = jnp.float32


def layer_kernel(
    snaps,
    ring,
    rows_ref,
    cols_ref,
    count_ref,
    feat,
    tiles_hbm,
    wg_hbm,
    gain_hbm,
    wq_hbm,
    wk_hbm,
    wv_hbm,
    wo_hbm,
    out,
    win_a,
    win_b,
    win_c,
    win_d,
    tiles,
    part,
    aggregated,
    resident_agg,
    resident_feat,
    mixed,
    hidden,
    query,
    key,
    value,
    wg,
    gain,
    wqkv,
    wo,
    gather_heads,
    spread_heads,
    normed,
    partial,
    wide,
    context,
    out_buf,
    prev_ref,
    last_ref,
    own_send,
    own_recv,
    relay_send,
    relay_recv,
    feat_send,
    feat_recv,
    agg_send,
    agg_recv,
    local_sem,
    out_sem,
):
    win = (win_a, win_b, win_c, win_d)
    blocks = feat.shape[0]
    tile = feat.shape[1]
    width = feat.shape[2]
    chunks = width // LANES
    group = LANES // HEADS
    period = snaps * HEADS
    slots = tiles.shape[0]
    s = lax.axis_index("snap")
    j = lax.axis_index("node")
    right = lax.rem(j + 1, ring)
    left = lax.rem(j + ring - 1, ring)
    node_peer = (right, left)
    near = (blocks, 3 * blocks)
    far = (0, 4 * blocks)

    def cols_of(c):
        return pl.ds(c * LANES, LANES)

    local = [pltpu.make_async_copy(tiles_hbm, tiles, local_sem.at[0])]
    for c in range(chunks):
        local.append(
            pltpu.make_async_copy(
                feat.at[:, :, cols_of(c)], win[c].at[pl.ds(2 * blocks, blocks)], local_sem.at[1 + c]
            )
        )
    base = 1 + chunks
    weights = [
        pltpu.make_async_copy(wg_hbm, wg, local_sem.at[base]),
        pltpu.make_async_copy(gain_hbm, gain, local_sem.at[base + 1]),
        pltpu.make_async_copy(wq_hbm, wqkv.at[0], local_sem.at[base + 2]),
        pltpu.make_async_copy(wk_hbm, wqkv.at[1], local_sem.at[base + 3]),
        pltpu.make_async_copy(wv_hbm, wqkv.at[2], local_sem.at[base + 4]),
        pltpu.make_async_copy(wo_hbm, wo, local_sem.at[base + 5]),
        pltpu.make_async_copy(feat.at[s], resident_feat.at[s], local_sem.at[base + 6]),
    ]

    def own(c, d):
        return pltpu.make_async_remote_copy(
            src_ref=feat.at[:, :, cols_of(c)],
            dst_ref=win[c].at[pl.ds(near[d], blocks)],
            send_sem=own_send.at[d, c],
            recv_sem=own_recv.at[d, c],
            device_id=(s, node_peer[d]),
            device_id_type=MESH,
        )

    def relay(c, d):
        return pltpu.make_async_remote_copy(
            src_ref=win[c].at[pl.ds(near[d], blocks)],
            dst_ref=win[c].at[pl.ds(far[d], blocks)],
            send_sem=relay_send.at[d, c],
            recv_sem=relay_recv.at[d, c],
            device_id=(s, node_peer[d]),
            device_id_type=MESH,
        )

    def feat_to(d):
        p = lax.rem(s + d, snaps)
        return pltpu.make_async_remote_copy(
            src_ref=feat.at[p],
            dst_ref=resident_feat.at[s],
            send_sem=feat_send.at[d - 1],
            recv_sem=feat_recv.at[d - 1],
            device_id=(p, j),
            device_id_type=MESH,
        )

    def agg_to(c, d):
        p = lax.rem(s + d, snaps)
        return pltpu.make_async_remote_copy(
            src_ref=aggregated.at[c, p],
            dst_ref=resident_agg.at[c, s],
            send_sem=agg_send.at[c, d - 1],
            recv_sem=agg_recv.at[c, d - 1],
            device_id=(p, j),
            device_id_type=MESH,
        )

    barrier = pltpu.get_barrier_semaphore()
    for d in range(2):
        pl.semaphore_signal(barrier, inc=1, device_id=(s, node_peer[d]), device_id_type=MESH)
    for d in range(1, snaps):
        pl.semaphore_signal(barrier, inc=1, device_id=(lax.rem(s + d, snaps), j), device_id_type=MESH)
    for copy in local:
        copy.start()
    pl.semaphore_wait(barrier, 1 + snaps)

    for c in range(2):
        for d in range(2):
            own(c, d).start()
    for copy in weights:
        copy.start()
    for d in range(1, snaps):
        feat_to(d).start()

    live_slots = count_ref[0, 0]

    def link(t, last):
        row = rows_ref[0, t] - j * blocks
        before = jnp.int32(0)
        for r in range(blocks):
            before = jnp.where(row == r, last[r], before)
        prev_ref[t] = before
        live = t < live_slots
        return tuple(jnp.where((row == r) & live, t + 1, last[r]) for r in range(blocks))

    last = lax.fori_loop(0, slots, link, (jnp.int32(0),) * blocks)
    for r in range(blocks):
        last_ref[r] = last[r]

    place = lax.broadcasted_iota(jnp.int32, (width, width), 1)
    source = lax.broadcasted_iota(jnp.int32, (width, width), 0)
    moved = lax.rem(place, HEADS) * HEAD_DIM + place // LANES * group + lax.rem(place, LANES) // HEADS
    order = jnp.where(source == moved, 1.0, 0.0).astype(BF16)
    moved = lax.rem(source, HEADS) * HEAD_DIM + source // LANES * group + lax.rem(source, LANES) // HEADS
    order_back = jnp.where(place == moved, 1.0, 0.0).astype(BF16)
    lane = lax.broadcasted_iota(jnp.int32, (snaps * LANES, LANES), 1)
    row = lax.broadcasted_iota(jnp.int32, (snaps * LANES, LANES), 0)
    hit = lax.rem(lane, period) == row // LANES * HEADS + lax.rem(row, HEADS)
    gather_heads[...] = jnp.where(hit, HEAD_DIM**-0.5, 0.0).astype(BF16)
    lane = lax.broadcasted_iota(jnp.int32, (LANES, snaps * LANES), 1)
    row = lax.broadcasted_iota(jnp.int32, (LANES, snaps * LANES), 0)
    hit = row == lane // LANES * HEADS + lax.rem(lane, HEADS)
    spread_heads[...] = jnp.where(hit, 1.0, 0.0).astype(BF16)
    partial[...] = jnp.zeros(partial.shape, BF16)
    for copy in weights:
        copy.wait()
    for i in range(3):
        wqkv[i] = jnp.dot(wqkv[i], order, preferred_element_type=F32).astype(BF16)
    wo[...] = jnp.dot(order_back, wo[...], preferred_element_type=F32).astype(BF16)
    part[0] = jnp.zeros((tile, LANES), F32)

    def aggregate(c):
        def product(t, carry):
            column = jnp.clip(cols_ref[0, t] - (j - 2) * blocks, 0, 5 * blocks - 1)
            part[t + 1] = jnp.dot(tiles[t], win[c][column], preferred_element_type=F32)
            return carry

        def step(i, carry):
            for k in range(4):
                product(i * 4 + k, carry)
            return carry

        lax.fori_loop(0, slots // 4, step, 0)
        for t in range(slots // 4 * 4, slots):
            product(t, 0)

        def chain(t, carry):
            part[t + 1] = part[t + 1] + part[prev_ref[t]]
            return carry

        lax.fori_loop(0, slots, chain, 0)
        for r in range(blocks):
            aggregated[c, r] = part[last_ref[r]].astype(BF16)
        for d in range(1, snaps):
            agg_to(c, d).start()
        resident_agg[c, s] = aggregated[c, s]

    for copy in local:
        copy.wait()

    def pass_on(c):
        for d in range(2):
            own(c, d).wait_recv()
            relay(c, d).start()
            if c + 2 < chunks:
                own(c + 2, d).start()

    def arrived(c):
        for d in range(2):
            relay(c, d).wait_recv()

    pass_on(0)
    pass_on(1)
    for c in range(chunks):
        arrived(c)
        aggregate(c)
        if c + 2 < chunks:
            pass_on(c + 2)
        if c == chunks - 2:
            for c2 in range(2):
                for d in range(1, snaps):
                    agg_to(c2, d).wait_recv()
            for u in range(snaps):
                pair = jnp.concatenate([resident_agg[0, u], resident_agg[1, u]], axis=1)
                mixed[u] = jnp.dot(pair, wg[pl.ds(0, 2 * LANES)], preferred_element_type=F32)

    for d in range(1, snaps):
        feat_to(d).wait_recv()
    for c2 in range(2, chunks):
        for d in range(1, snaps):
            agg_to(c2, d).wait_recv()

    half = snaps // 2
    rows = half * tile
    for h in range(2):
        for t in range(h * half, (h + 1) * half):
            pair = jnp.concatenate([resident_agg[2, t], resident_agg[3, t]], axis=1)
            total = mixed[t] + jnp.dot(pair, wg[pl.ds(2 * LANES, 2 * LANES)], preferred_element_type=F32)
            hid = (resident_feat[t].astype(F32) + jnp.maximum(total, 0.0)).astype(BF16)
            hidden[t] = hid
            hid = hid.astype(F32)
            mean = jnp.mean(hid, axis=-1, keepdims=True)
            centred = hid - mean
            variance = jnp.mean(centred * centred, axis=-1, keepdims=True)
            normed[t] = (centred * lax.rsqrt(variance + 1e-05) * gain[...]).astype(BF16)
        part_of = pl.ds(h * half, half)
        some = normed[part_of].reshape(rows, width)
        for i, to in enumerate((query, key, value)):
            product = jnp.dot(some, wqkv[i], preferred_element_type=F32).astype(BF16).astype(F32)
            to[part_of] = product.reshape(half, tile, width)

    def column(u):
        return pl.ds(u * LANES, LANES)

    def score_rows(i, carry):
        at = pl.ds(pl.multiple_of(i * 16, 16), 16)
        for t in range(snaps):
            for u in range(t + 1):
                total = query[t, at, column(0)] * key[u, at, column(0)]
                for v in range(1, chunks):
                    total = total + query[t, at, column(v)] * key[u, at, column(v)]
                partial[t, at, column(u)] = total.astype(BF16)
        return carry

    lax.fori_loop(0, tile // 16, score_rows, 0)

    lane = lax.broadcasted_iota(jnp.int32, (snaps, tile, LANES), 2)
    of_row = lax.broadcasted_iota(jnp.int32, (snaps, tile, LANES), 0)
    visible = (lax.rem(lane, period) // HEADS <= of_row).reshape(snaps * tile, LANES)
    scores = jnp.dot(
        partial[...].reshape(snaps * tile, snaps * LANES), gather_heads[...], preferred_element_type=F32
    )
    scores = jnp.where(visible, scores, -1e30)
    top = scores
    shift = HEADS
    while shift < period:
        top = jnp.maximum(top, pltpu.roll(top, shift, 1))
        shift *= 2
    e = jnp.exp(scores - top)
    total = e
    shift = HEADS
    while shift < period:
        total = total + pltpu.roll(total, shift, 1)
        shift *= 2
    w = (e / total).astype(BF16)
    wide[...] = jnp.dot(w, spread_heads[...], preferred_element_type=F32).reshape(wide.shape)

    def context_rows(i, carry):
        at = pl.ds(pl.multiple_of(i * 16, 16), 16)
        for t in range(snaps):
            for v in range(chunks):
                total = wide[t, at, column(0)] * value[0, at, column(v)]
                for u in range(1, t + 1):
                    total = total + wide[t, at, column(u)] * value[u, at, column(v)]
                context[t, at, column(v)] = total.astype(BF16)
        return carry

    lax.fori_loop(0, tile // 16, context_rows, 0)

    for h in range(2):
        part_of = pl.ds(h * half, half)
        projected = jnp.dot(context[part_of].reshape(rows, width), wo[...], preferred_element_type=F32)
        result = hidden[part_of].astype(F32) + projected.reshape(half, tile, width)
        out_buf[part_of] = result.astype(BF16)
        pltpu.make_async_copy(out_buf.at[part_of], out.at[part_of], out_sem.at[h]).start()

    for c in range(chunks):
        for d in range(2):
            own(c, d).wait_send()
            relay(c, d).wait_send()
        for d in range(1, snaps):
            agg_to(c, d).wait_send()
    for d in range(1, snaps):
        feat_to(d).wait_send()
    for h in range(2):
        part_of = pl.ds(h * half, half)
        pltpu.make_async_copy(out_buf.at[part_of], out.at[part_of], out_sem.at[h]).wait()


def local_layer(
    snaps,
    ring,
    features,
    tile_rows,
    tile_cols,
    tile_values,
    tile_count,
    w_graph,
    norm_gain,
    w_query,
    w_key,
    w_value,
    w_out,
):
    nodes_dev, width = features.shape[1:]
    slots, tile = tile_values.shape[1:3]
    blocks = nodes_dev // tile
    chunks = width // LANES
    smem = pl.BlockSpec(memory_space=pltpu.SMEM)
    hbm = pl.BlockSpec(memory_space=pltpu.HBM)
    dma = pltpu.SemaphoreType.DMA

    def kernel(*refs):
        layer_kernel(snaps, ring, *refs)

    return pl.pallas_call(
        kernel,
        out_shape=jax.ShapeDtypeStruct((snaps, tile, width), BF16),
        in_specs=[smem] * 3 + [hbm] * 8,
        out_specs=hbm,
        scratch_shapes=[
            *[pltpu.VMEM((5 * blocks, tile, LANES), BF16)] * chunks,
            pltpu.VMEM((slots, tile, tile), BF16),
            pltpu.VMEM((slots + 1, tile, LANES), F32),
            pltpu.VMEM((chunks, blocks, tile, LANES), BF16),
            pltpu.VMEM((chunks, snaps, tile, LANES), BF16),
            pltpu.VMEM((snaps, tile, width), BF16),
            pltpu.VMEM((snaps, tile, width), F32),
            pltpu.VMEM((snaps, tile, width), BF16),
            pltpu.VMEM((snaps, tile, width), F32),
            pltpu.VMEM((snaps, tile, width), F32),
            pltpu.VMEM((snaps, tile, width), F32),
            pltpu.VMEM((width, width), BF16),
            pltpu.VMEM((1, width), F32),
            pltpu.VMEM((3, width, width), BF16),
            pltpu.VMEM((width, width), BF16),
            pltpu.VMEM((snaps * LANES, LANES), BF16),
            pltpu.VMEM((LANES, snaps * LANES), BF16),
            pltpu.VMEM((snaps, tile, width), BF16),
            pltpu.VMEM((snaps, tile, snaps * LANES), BF16),
            pltpu.VMEM((snaps, tile, snaps * LANES), F32),
            pltpu.VMEM((snaps, tile, width), BF16),
            pltpu.VMEM((snaps, tile, width), BF16),
            pltpu.SMEM((slots,), jnp.int32),
            pltpu.SMEM((blocks,), jnp.int32),
            dma((2, chunks)),
            dma((2, chunks)),
            dma((2, chunks)),
            dma((2, chunks)),
            dma((snaps - 1,)),
            dma((snaps - 1,)),
            dma((chunks, snaps - 1)),
            dma((chunks, snaps - 1)),
            dma((8 + chunks,)),
            dma((snaps,)),
        ],
        compiler_params=pltpu.CompilerParams(
            collective_id=0, has_side_effects=True, vmem_limit_bytes=60 * 2**20
        ),
        cost_estimate=pl.CostEstimate(
            flops=4 * 10**9, bytes_accessed=6 * 2**20, transcendentals=10**6
        ),
    )(
        tile_rows,
        tile_cols,
        tile_count,
        features.reshape(blocks, tile, width),
        tile_values[0],
        w_graph,
        norm_gain.reshape(1, width),
        w_query,
        w_key,
        w_value,
        w_out,
    )


def solution(mesh):
    snaps, ring = mesh.shape["snap"], mesh.shape["node"]

    def local(*args):
        return local_layer(snaps, ring, *args)

    in_specs = (
        P("snap", "node", None),
        P("snap", "node"),
        P("snap", "node"),
        P("snap", "node", None, None),
        P("snap", "node"),
        P(),
        P(),
        P(),
        P(),
        P(),
        P(),
    )
    return jax.shard_map(
        local, mesh=mesh, in_specs=in_specs, out_specs=P(None, ("node", "snap"), None), check_vma=False
    )
```

```python
import jax
import jax.numpy as jnp
from jax import lax
from jax.experimental import pallas as pl
from jax.experimental.pallas import tpu as pltpu
from jax.sharding import PartitionSpec as P

MESH = pl.DeviceIdType.MESH
HEADS = 8
HEAD_DIM = 64
LANES = 128
BF16 = jnp.bfloat16
F32 = jnp.float32


def layer_kernel(
    snaps,
    ring,
    rows_ref,
    cols_ref,
    count_ref,
    feat,
    tiles_hbm,
    wg_hbm,
    gain_hbm,
    wq_hbm,
    wk_hbm,
    wv_hbm,
    wo_hbm,
    out,
    win_a,
    win_b,
    win_c,
    win_d,
    tiles,
    part,
    aggregated,
    resident_agg,
    resident_feat,
    mixed,
    hidden,
    query,
    key,
    value,
    wg,
    gain,
    wqkv,
    wo,
    gather_heads,
    spread_heads,
    partial,
    wide,
    context,
    out_buf,
    key_ref,
    rank_ref,
    slot_ref,
    column_ref,
    keep_ref,
    last_ref,
    own_send,
    own_recv,
    relay_send,
    relay_recv,
    feat_send,
    feat_recv,
    agg_send,
    agg_recv,
    local_sem,
    out_sem,
):
    win = (win_a, win_b, win_c, win_d)
    blocks = feat.shape[0]
    tile = feat.shape[1]
    width = feat.shape[2]
    chunks = width // LANES
    group = LANES // HEADS
    period = snaps * HEADS
    slots = tiles.shape[0]
    s = lax.axis_index("snap")
    j = lax.axis_index("node")
    right = lax.rem(j + 1, ring)
    left = lax.rem(j + ring - 1, ring)
    node_peer = (right, left)
    has_left, has_right = j > 0, j < ring - 1
    has_both = has_left & has_right
    sends, receives = (has_right, has_left), (has_left, has_right)
    receives_far = (j > 1, j < ring - 2)
    near = (blocks, 3 * blocks)
    far = (0, 4 * blocks)

    def cols_of(c):
        return pl.ds(c * LANES, LANES)

    local = [pltpu.make_async_copy(tiles_hbm, tiles, local_sem.at[0])]
    for c in range(chunks):
        local.append(
            pltpu.make_async_copy(
                feat.at[:, :, cols_of(c)], win[c].at[pl.ds(2 * blocks, blocks)], local_sem.at[1 + c]
            )
        )
    base = 1 + chunks
    weights = [
        pltpu.make_async_copy(wg_hbm, wg, local_sem.at[base]),
        pltpu.make_async_copy(gain_hbm, gain, local_sem.at[base + 1]),
        pltpu.make_async_copy(wq_hbm, wqkv.at[0], local_sem.at[base + 2]),
        pltpu.make_async_copy(wk_hbm, wqkv.at[1], local_sem.at[base + 3]),
        pltpu.make_async_copy(wv_hbm, wqkv.at[2], local_sem.at[base + 4]),
        pltpu.make_async_copy(wo_hbm, wo, local_sem.at[base + 5]),
        pltpu.make_async_copy(feat.at[s], resident_feat.at[s], local_sem.at[base + 6]),
    ]

    def own(c, d):
        return pltpu.make_async_remote_copy(
            src_ref=feat.at[:, :, cols_of(c)],
            dst_ref=win[c].at[pl.ds(near[d], blocks)],
            send_sem=own_send.at[d, c],
            recv_sem=own_recv.at[d, c],
            device_id=(s, node_peer[d]),
            device_id_type=MESH,
        )

    def relay(c, d):
        return pltpu.make_async_remote_copy(
            src_ref=win[c].at[pl.ds(near[d], blocks)],
            dst_ref=win[c].at[pl.ds(far[d], blocks)],
            send_sem=relay_send.at[d, c],
            recv_sem=relay_recv.at[d, c],
            device_id=(s, node_peer[d]),
            device_id_type=MESH,
        )

    def feat_with(p):
        return pltpu.make_async_remote_copy(
            src_ref=feat.at[p],
            dst_ref=resident_feat.at[s],
            send_sem=feat_send.at[p],
            recv_sem=feat_recv.at[s],
            device_id=(p, j),
            device_id_type=MESH,
        )

    def feat_from(p):
        return pltpu.make_async_remote_copy(
            src_ref=feat.at[p],
            dst_ref=resident_feat.at[p],
            send_sem=feat_send.at[p],
            recv_sem=feat_recv.at[p],
            device_id=(p, j),
            device_id_type=MESH,
        )

    def agg_with(c, p):
        return pltpu.make_async_remote_copy(
            src_ref=aggregated.at[c, p],
            dst_ref=resident_agg.at[c, s],
            send_sem=agg_send.at[c, p],
            recv_sem=agg_recv.at[c, s],
            device_id=(p, j),
            device_id_type=MESH,
        )

    def agg_from(c, p):
        return pltpu.make_async_remote_copy(
            src_ref=aggregated.at[c, p],
            dst_ref=resident_agg.at[c, p],
            send_sem=agg_send.at[c, p],
            recv_sem=agg_recv.at[c, p],
            device_id=(p, j),
            device_id_type=MESH,
        )

    chips = snaps // 2
    chip = lax.div(s, 2)
    other_core = s + 1 - 2 * lax.rem(s, 2)
    pair_of = [2 * lax.rem(chip + g, chips) for g in range(chips)]
    near_first = (0, 1, 3, 2)
    peers = [pair_of[g] + k for g in (2, 1, 3) for k in range(2)] + [other_core]

    barrier = pltpu.get_barrier_semaphore()
    for d in range(2):

        @pl.when(sends[d])
        def _():
            pl.semaphore_signal(barrier, inc=1, device_id=(s, node_peer[d]), device_id_type=MESH)

    for p in peers:
        pl.semaphore_signal(barrier, inc=1, device_id=(p, j), device_id_type=MESH)
    for copy in local:
        copy.start()
    for copy in weights:
        copy.start()
    pl.semaphore_wait(
        barrier, snaps - 1 + has_left.astype(jnp.int32) + has_right.astype(jnp.int32)
    )

    def start_own(c, d):
        @pl.when(sends[d])
        def _():
            own(c, d).start()

    for c in range(2):
        for d in range(2):
            start_own(c, d)
    for p in peers:
        feat_with(p).start()

    live_slots = count_ref[0, 0]

    def find_key(t, carry):
        key_ref[t] = jnp.where(t < live_slots, rows_ref[0, t] - j * blocks, blocks)
        return carry

    def find_rank(t, carry):
        mine = key_ref[t]
        rank = jnp.int32(0)
        for o in range(slots):
            theirs = key_ref[o]
            ahead = (theirs < mine) | ((theirs == mine) & (o < t))
            rank = rank + ahead.astype(jnp.int32)
        rank_ref[t] = rank
        return carry

    def find_slot(p, last):
        slot = jnp.int32(0)
        for o in range(slots):
            slot = jnp.where(rank_ref[o] == p, o, slot)
        slot_ref[p] = slot
        row = key_ref[slot]
        column_ref[p] = jnp.clip(cols_ref[0, slot] - (j - 2) * blocks, 0, 5 * blocks - 1)
        keep_ref[p] = jnp.where(row == last[blocks], 1.0, 0.0)
        ends = tuple(jnp.where(row == r, p + 1, last[r]) for r in range(blocks))
        return ends + (row,)

    lax.fori_loop(0, slots, find_key, 0)
    lax.fori_loop(0, slots, find_rank, 0)
    last = lax.fori_loop(0, slots, find_slot, (jnp.int32(0),) * blocks + (jnp.int32(-1),))
    for r in range(blocks):
        last_ref[r] = last[r]

    place = lax.broadcasted_iota(jnp.int32, (width, width), 1)
    source = lax.broadcasted_iota(jnp.int32, (width, width), 0)
    moved = lax.rem(place, HEADS) * HEAD_DIM + place // LANES * group + lax.rem(place, LANES) // HEADS
    order = jnp.where(source == moved, 1.0, 0.0).astype(BF16)
    moved = lax.rem(source, HEADS) * HEAD_DIM + source // LANES * group + lax.rem(source, LANES) // HEADS
    order_back = jnp.where(place == moved, 1.0, 0.0).astype(BF16)
    lane = lax.broadcasted_iota(jnp.int32, (snaps * LANES, LANES), 1)
    row = lax.broadcasted_iota(jnp.int32, (snaps * LANES, LANES), 0)
    hit = lax.rem(lane, period) == row // LANES * HEADS + lax.rem(row, HEADS)
    gather_heads[...] = jnp.where(hit, HEAD_DIM**-0.5, 0.0).astype(BF16)
    lane = lax.broadcasted_iota(jnp.int32, (LANES, snaps * LANES), 1)
    row = lax.broadcasted_iota(jnp.int32, (LANES, snaps * LANES), 0)
    hit = row == lane // LANES * HEADS + lax.rem(lane, HEADS)
    spread_heads[...] = jnp.where(hit, 1.0, 0.0).astype(BF16)
    partial[...] = jnp.zeros(partial.shape, BF16)
    for copy in weights:
        copy.wait()
    for i in range(3):
        wqkv[i] = jnp.dot(wqkv[i], order, preferred_element_type=F32).astype(BF16)
    wo[...] = jnp.dot(order_back, wo[...], preferred_element_type=F32).astype(BF16)
    part[0] = jnp.zeros((tile, LANES), F32)

    def aggregate(c):
        def product(p, total):
            term = jnp.dot(tiles[slot_ref[p]], win[c][column_ref[p]], preferred_element_type=F32)
            total = total * keep_ref[p] + term
            part[p + 1] = total
            return total

        def step(i, total):
            for k in range(4):
                total = product(i * 4 + k, total)
            return total

        total = lax.fori_loop(0, slots // 4, step, jnp.zeros((tile, LANES), F32))
        for p in range(slots // 4 * 4, slots):
            total = product(p, total)
        for r in range(blocks):
            aggregated[c, r] = part[last_ref[r]].astype(BF16)
        for p in peers:
            agg_with(c, p).start()
        resident_agg[c, s] = aggregated[c, s]

    for copy in local:
        copy.wait()

    def pass_on(c):
        for d in range(2):

            @pl.when(receives[d])
            def _():
                own(c, d).wait_recv()

            @pl.when(has_both)
            def _():
                relay(c, d).start()

            if c + 2 < chunks:
                start_own(c + 2, d)

    def arrived(c):
        for d in range(2):

            @pl.when(receives_far[d])
            def _():
                relay(c, d).wait_recv()

    pass_on(0)
    pass_on(1)
    for c in range(chunks):
        arrived(c)
        aggregate(c)
        if c + 2 < chunks:
            pass_on(c + 2)
        if c == chunks - 2:
            for c2 in range(2):
                for p in peers:
                    agg_from(c2, p).wait_recv()
            for u in range(snaps):
                both = jnp.concatenate([resident_agg[0, u], resident_agg[1, u]], axis=1)
                mixed[u] = jnp.dot(both, wg[pl.ds(0, 2 * LANES)], preferred_element_type=F32)
            for p in peers:
                feat_from(p).wait_recv()

    rows = 2 * tile
    for g in near_first:
        for p in [other_core] if g == 0 else [pair_of[g], pair_of[g] + 1]:
            for c in range(2, chunks):
                agg_from(c, p).wait_recv()
        pair = pl.ds(pair_of[g], 2)
        both = jnp.concatenate(
            [resident_agg[c, pair].reshape(rows, LANES) for c in range(2, chunks)], axis=1
        )
        total = jnp.dot(both, wg[pl.ds(2 * LANES, 2 * LANES)], preferred_element_type=F32)
        total = mixed[pair].reshape(rows, width) + total
        hid = resident_feat[pair].reshape(rows, width).astype(F32) + jnp.maximum(total, 0.0)
        hid = hid.astype(BF16)
        hidden[pair] = hid.reshape(2, tile, width)
        hid = hid.astype(F32)
        mean = jnp.mean(hid, axis=-1, keepdims=True)
        centred = hid - mean
        variance = jnp.mean(centred * centred, axis=-1, keepdims=True)
        normed = (centred * lax.rsqrt(variance + 1e-05) * gain[...]).astype(BF16)
        for i, to in enumerate((query, key, value)):
            product = jnp.dot(normed, wqkv[i], preferred_element_type=F32).astype(BF16).astype(F32)
            to[pair] = product.reshape(2, tile, width)

    def column(u):
        return pl.ds(u * LANES, LANES)

    def score_rows(i, carry):
        at = pl.ds(pl.multiple_of(i * 16, 16), 16)
        for t in range(snaps):
            for u in range(t + 1):
                total = query[t, at, column(0)] * key[u, at, column(0)]
                for v in range(1, chunks):
                    total = total + query[t, at, column(v)] * key[u, at, column(v)]
                partial[t, at, column(u)] = total.astype(BF16)
        return carry

    lax.fori_loop(0, tile // 16, score_rows, 0)

    lane = lax.broadcasted_iota(jnp.int32, (snaps, tile, LANES), 2)
    of_row = lax.broadcasted_iota(jnp.int32, (snaps, tile, LANES), 0)
    visible = (lax.rem(lane, period) // HEADS <= of_row).reshape(snaps * tile, LANES)
    scores = jnp.dot(
        partial[...].reshape(snaps * tile, snaps * LANES), gather_heads[...], preferred_element_type=F32
    )
    scores = jnp.where(visible, scores, -1e30)
    top = scores
    shift = HEADS
    while shift < period:
        top = jnp.maximum(top, pltpu.roll(top, shift, 1))
        shift *= 2
    e = jnp.exp(scores - top)
    total = e
    shift = HEADS
    while shift < period:
        total = total + pltpu.roll(total, shift, 1)
        shift *= 2
    w = (e / total).astype(BF16)
    wide[...] = jnp.dot(w, spread_heads[...], preferred_element_type=F32).reshape(wide.shape)

    def context_rows(i, carry):
        at = pl.ds(pl.multiple_of(i * 16, 16), 16)
        for t in range(snaps):
            for v in range(chunks):
                total = wide[t, at, column(0)] * value[0, at, column(v)]
                for u in range(1, t + 1):
                    total = total + wide[t, at, column(u)] * value[u, at, column(v)]
                context[t, at, column(v)] = total.astype(BF16)
        return carry

    lax.fori_loop(0, tile // 16, context_rows, 0)

    half = snaps // 2
    rows = half * tile
    for h in range(2):
        part_of = pl.ds(h * half, half)
        projected = jnp.dot(context[part_of].reshape(rows, width), wo[...], preferred_element_type=F32)
        result = hidden[part_of].astype(F32) + projected.reshape(half, tile, width)
        out_buf[part_of] = result.astype(BF16)
        pltpu.make_async_copy(out_buf.at[part_of], out.at[part_of], out_sem.at[h]).start()

    for c in range(chunks):
        for d in range(2):

            @pl.when(sends[d])
            def _():
                own(c, d).wait_send()

            @pl.when(has_both)
            def _():
                relay(c, d).wait_send()

        for p in peers:
            agg_with(c, p).wait_send()
    for p in peers:
        feat_with(p).wait_send()
    for h in range(2):
        part_of = pl.ds(h * half, half)
        pltpu.make_async_copy(out_buf.at[part_of], out.at[part_of], out_sem.at[h]).wait()


def local_layer(
    snaps,
    ring,
    features,
    tile_rows,
    tile_cols,
    tile_values,
    tile_count,
    w_graph,
    norm_gain,
    w_query,
    w_key,
    w_value,
    w_out,
):
    nodes_dev, width = features.shape[1:]
    slots, tile = tile_values.shape[1:3]
    blocks = nodes_dev // tile
    chunks = width // LANES
    smem = pl.BlockSpec(memory_space=pltpu.SMEM)
    hbm = pl.BlockSpec(memory_space=pltpu.HBM)
    dma = pltpu.SemaphoreType.DMA

    def kernel(*refs):
        layer_kernel(snaps, ring, *refs)

    return pl.pallas_call(
        kernel,
        out_shape=jax.ShapeDtypeStruct((snaps, tile, width), BF16),
        in_specs=[smem] * 3 + [hbm] * 8,
        out_specs=hbm,
        scratch_shapes=[
            *[pltpu.VMEM((5 * blocks, tile, LANES), BF16)] * chunks,
            pltpu.VMEM((slots, tile, tile), BF16),
            pltpu.VMEM((slots + 1, tile, LANES), F32),
            pltpu.VMEM((chunks, blocks, tile, LANES), BF16),
            pltpu.VMEM((chunks, snaps, tile, LANES), BF16),
            pltpu.VMEM((snaps, tile, width), BF16),
            pltpu.VMEM((snaps, tile, width), F32),
            pltpu.VMEM((snaps, tile, width), BF16),
            pltpu.VMEM((snaps, tile, width), F32),
            pltpu.VMEM((snaps, tile, width), F32),
            pltpu.VMEM((snaps, tile, width), F32),
            pltpu.VMEM((width, width), BF16),
            pltpu.VMEM((1, width), F32),
            pltpu.VMEM((3, width, width), BF16),
            pltpu.VMEM((width, width), BF16),
            pltpu.VMEM((snaps * LANES, LANES), BF16),
            pltpu.VMEM((LANES, snaps * LANES), BF16),
            pltpu.VMEM((snaps, tile, snaps * LANES), BF16),
            pltpu.VMEM((snaps, tile, snaps * LANES), F32),
            pltpu.VMEM((snaps, tile, width), BF16),
            pltpu.VMEM((snaps, tile, width), BF16),
            *[pltpu.SMEM((slots,), jnp.int32)] * 4,
            pltpu.SMEM((slots,), F32),
            pltpu.SMEM((blocks,), jnp.int32),
            dma((2, chunks)),
            dma((2, chunks)),
            dma((2, chunks)),
            dma((2, chunks)),
            dma((snaps,)),
            dma((snaps,)),
            dma((chunks, snaps)),
            dma((chunks, snaps)),
            dma((8 + chunks,)),
            dma((snaps,)),
        ],
        compiler_params=pltpu.CompilerParams(
            collective_id=0, has_side_effects=True, vmem_limit_bytes=60 * 2**20
        ),
        cost_estimate=pl.CostEstimate(
            flops=4 * 10**9, bytes_accessed=6 * 2**20, transcendentals=10**6
        ),
    )(
        tile_rows,
        tile_cols,
        tile_count,
        features.reshape(blocks, tile, width),
        tile_values[0],
        w_graph,
        norm_gain.reshape(1, width),
        w_query,
        w_key,
        w_value,
        w_out,
    )


def solution(mesh):
    snaps, ring = mesh.shape["snap"], mesh.shape["node"]

    def local(*args):
        return local_layer(snaps, ring, *args)

    in_specs = (
        P("snap", "node", None),
        P("snap", "node"),
        P("snap", "node"),
        P("snap", "node", None, None),
        P("snap", "node"),
        P(),
        P(),
        P(),
        P(),
        P(),
        P(),
    )
    return jax.shard_map(
        local, mesh=mesh, in_specs=in_specs, out_specs=P(None, ("node", "snap"), None), check_vma=False
    )
```

```python
import jax
import jax.numpy as jnp
from jax import lax
from jax.experimental import pallas as pl
from jax.experimental.pallas import tpu as pltpu
from jax.sharding import PartitionSpec as P

MESH = pl.DeviceIdType.MESH
HEADS = 8
HEAD_DIM = 64
LANES = 128
BF16 = jnp.bfloat16
F32 = jnp.float32


def layer_kernel(
    snaps,
    ring,
    rows_ref,
    cols_ref,
    count_ref,
    feat,
    tiles_hbm,
    wg_hbm,
    gain_hbm,
    wq_hbm,
    wk_hbm,
    wv_hbm,
    wo_hbm,
    out,
    win_a,
    win_b,
    win_c,
    win_d,
    tiles,
    part,
    aggregated,
    resident_agg,
    resident_feat,
    mixed,
    hidden,
    query,
    key,
    value,
    wg,
    gain,
    wqkv,
    wo,
    head_sum,
    partial,
    scores,
    context,
    key_ref,
    rank_ref,
    slot_ref,
    column_ref,
    keep_ref,
    last_ref,
    own_send,
    own_recv,
    relay_send,
    relay_recv,
    feat_send,
    feat_recv,
    agg_send,
    agg_recv,
    local_sem,
):
    win = (win_a, win_b, win_c, win_d)
    blocks = feat.shape[0]
    tile = feat.shape[1]
    width = feat.shape[2]
    chunks = width // LANES
    group = LANES // HEADS
    slots = tiles.shape[0]
    s = lax.axis_index("snap")
    j = lax.axis_index("node")
    right = lax.rem(j + 1, ring)
    left = lax.rem(j + ring - 1, ring)
    node_peer = (right, left)
    has_left, has_right = j > 0, j < ring - 1
    has_both = has_left & has_right
    sends, receives = (has_right, has_left), (has_left, has_right)
    receives_far = (j > 1, j < ring - 2)
    near = (blocks, 3 * blocks)
    far = (0, 4 * blocks)

    def cols_of(c):
        return pl.ds(c * LANES, LANES)

    local = [pltpu.make_async_copy(tiles_hbm, tiles, local_sem.at[0])]
    for c in range(chunks):
        local.append(
            pltpu.make_async_copy(
                feat.at[:, :, cols_of(c)], win[c].at[pl.ds(2 * blocks, blocks)], local_sem.at[1 + c]
            )
        )
    base = 1 + chunks
    weights = [
        pltpu.make_async_copy(wg_hbm, wg, local_sem.at[base]),
        pltpu.make_async_copy(gain_hbm, gain, local_sem.at[base + 1]),
        pltpu.make_async_copy(wq_hbm, wqkv.at[0], local_sem.at[base + 2]),
        pltpu.make_async_copy(wk_hbm, wqkv.at[1], local_sem.at[base + 3]),
        pltpu.make_async_copy(wv_hbm, wqkv.at[2], local_sem.at[base + 4]),
        pltpu.make_async_copy(wo_hbm, wo, local_sem.at[base + 5]),
        pltpu.make_async_copy(feat.at[s], resident_feat.at[s], local_sem.at[base + 6]),
    ]

    def own(c, d):
        return pltpu.make_async_remote_copy(
            src_ref=feat.at[:, :, cols_of(c)],
            dst_ref=win[c].at[pl.ds(near[d], blocks)],
            send_sem=own_send.at[d, c],
            recv_sem=own_recv.at[d, c],
            device_id=(s, node_peer[d]),
            device_id_type=MESH,
        )

    def relay(c, d):
        return pltpu.make_async_remote_copy(
            src_ref=win[c].at[pl.ds(near[d], blocks)],
            dst_ref=win[c].at[pl.ds(far[d], blocks)],
            send_sem=relay_send.at[d, c],
            recv_sem=relay_recv.at[d, c],
            device_id=(s, node_peer[d]),
            device_id_type=MESH,
        )

    def feat_with(p):
        return pltpu.make_async_remote_copy(
            src_ref=feat.at[p],
            dst_ref=resident_feat.at[s],
            send_sem=feat_send.at[p],
            recv_sem=feat_recv.at[s],
            device_id=(p, j),
            device_id_type=MESH,
        )

    def feat_from(p):
        return pltpu.make_async_remote_copy(
            src_ref=feat.at[p],
            dst_ref=resident_feat.at[p],
            send_sem=feat_send.at[p],
            recv_sem=feat_recv.at[p],
            device_id=(p, j),
            device_id_type=MESH,
        )

    def agg_with(c, p):
        return pltpu.make_async_remote_copy(
            src_ref=aggregated.at[c, p],
            dst_ref=resident_agg.at[c, s],
            send_sem=agg_send.at[c, p],
            recv_sem=agg_recv.at[c, s],
            device_id=(p, j),
            device_id_type=MESH,
        )

    def agg_from(c, p):
        return pltpu.make_async_remote_copy(
            src_ref=aggregated.at[c, p],
            dst_ref=resident_agg.at[c, p],
            send_sem=agg_send.at[c, p],
            recv_sem=agg_recv.at[c, p],
            device_id=(p, j),
            device_id_type=MESH,
        )

    chips = snaps // 2
    chip = lax.div(s, 2)
    other_core = s + 1 - 2 * lax.rem(s, 2)
    pair_of = [2 * lax.rem(chip + g, chips) for g in range(chips)]
    near_first = (0, 1, 3, 2)
    peers = [pair_of[g] + k for g in (2, 1, 3) for k in range(2)] + [other_core]

    barrier = pltpu.get_barrier_semaphore()
    for d in range(2):

        @pl.when(sends[d])
        def _():
            pl.semaphore_signal(barrier, inc=1, device_id=(s, node_peer[d]), device_id_type=MESH)

    for p in peers:
        pl.semaphore_signal(barrier, inc=1, device_id=(p, j), device_id_type=MESH)
    for copy in local:
        copy.start()
    for copy in weights:
        copy.start()
    pl.semaphore_wait(
        barrier, snaps - 1 + has_left.astype(jnp.int32) + has_right.astype(jnp.int32)
    )

    def start_own(c, d):
        @pl.when(sends[d])
        def _():
            own(c, d).start()

    for c in range(2):
        for d in range(2):
            start_own(c, d)
    for p in peers:
        feat_with(p).start()

    live_slots = count_ref[0, 0]

    def find_key(t, carry):
        key_ref[t] = jnp.where(t < live_slots, rows_ref[0, t] - j * blocks, blocks)
        return carry

    def find_rank(t, carry):
        mine = key_ref[t]
        rank = jnp.int32(0)
        for o in range(slots):
            theirs = key_ref[o]
            ahead = (theirs < mine) | ((theirs == mine) & (o < t))
            rank = rank + ahead.astype(jnp.int32)
        rank_ref[t] = rank
        return carry

    def find_slot(p, last):
        slot = jnp.int32(0)
        for o in range(slots):
            slot = jnp.where(rank_ref[o] == p, o, slot)
        slot_ref[p] = slot
        row = key_ref[slot]
        column_ref[p] = jnp.clip(cols_ref[0, slot] - (j - 2) * blocks, 0, 5 * blocks - 1)
        keep_ref[p] = jnp.where(row == last[blocks], 1.0, 0.0)
        ends = tuple(jnp.where(row == r, p + 1, last[r]) for r in range(blocks))
        return ends + (row,)

    lax.fori_loop(0, slots, find_key, 0)
    lax.fori_loop(0, slots, find_rank, 0)
    last = lax.fori_loop(0, slots, find_slot, (jnp.int32(0),) * blocks + (jnp.int32(-1),))
    for r in range(blocks):
        last_ref[r] = last[r]

    place = lax.broadcasted_iota(jnp.int32, (width, width), 1)
    source = lax.broadcasted_iota(jnp.int32, (width, width), 0)
    moved = lax.rem(place, HEADS) * HEAD_DIM + place // LANES * group + lax.rem(place, LANES) // HEADS
    order = jnp.where(source == moved, 1.0, 0.0).astype(BF16)
    moved = lax.rem(source, HEADS) * HEAD_DIM + source // LANES * group + lax.rem(source, LANES) // HEADS
    order_back = jnp.where(place == moved, 1.0, 0.0).astype(BF16)
    lane = lax.broadcasted_iota(jnp.int32, (2 * LANES, 2 * LANES), 1)
    row = lax.broadcasted_iota(jnp.int32, (2 * LANES, 2 * LANES), 0)
    hit = (lane // LANES == row // LANES) & (lax.rem(lane, HEADS) == lax.rem(row, HEADS))
    head_sum[...] = jnp.where(hit, HEAD_DIM**-0.5, 0.0).astype(BF16)
    partial[...] = jnp.zeros(partial.shape, BF16)
    for copy in weights:
        copy.wait()
    for i in range(3):
        wqkv[i] = jnp.dot(wqkv[i], order, preferred_element_type=F32).astype(BF16)
    wo[...] = jnp.dot(order_back, wo[...], preferred_element_type=F32).astype(BF16)
    part[0] = jnp.zeros((tile, LANES), F32)

    def aggregate(c):
        def product(p, total):
            term = jnp.dot(tiles[slot_ref[p]], win[c][column_ref[p]], preferred_element_type=F32)
            total = total * keep_ref[p] + term
            part[p + 1] = total
            return total

        def step(i, total):
            for k in range(4):
                total = product(i * 4 + k, total)
            return total

        total = lax.fori_loop(0, slots // 4, step, jnp.zeros((tile, LANES), F32))
        for p in range(slots // 4 * 4, slots):
            total = product(p, total)
        for r in range(blocks):
            aggregated[c, r] = part[last_ref[r]].astype(BF16)
        for p in peers:
            agg_with(c, p).start()
        resident_agg[c, s] = aggregated[c, s]

    for copy in local:
        copy.wait()

    def pass_on(c):
        for d in range(2):

            @pl.when(receives[d])
            def _():
                own(c, d).wait_recv()

            @pl.when(has_both)
            def _():
                relay(c, d).start()

            if c + 2 < chunks:
                start_own(c + 2, d)

    def arrived(c):
        for d in range(2):

            @pl.when(receives_far[d])
            def _():
                relay(c, d).wait_recv()

    pass_on(0)
    pass_on(1)
    for c in range(chunks):
        arrived(c)
        aggregate(c)
        if c + 2 < chunks:
            pass_on(c + 2)
        if c == chunks - 2:
            for c2 in range(2):
                for p in peers:
                    agg_from(c2, p).wait_recv()
            for u in range(snaps):
                both = jnp.concatenate([resident_agg[0, u], resident_agg[1, u]], axis=1)
                mixed[u] = jnp.dot(both, wg[pl.ds(0, 2 * LANES)], preferred_element_type=F32)
            for p in peers:
                feat_from(p).wait_recv()

    rows = 2 * tile
    for g in near_first:
        for p in [other_core] if g == 0 else [pair_of[g], pair_of[g] + 1]:
            for c in range(2, chunks):
                agg_from(c, p).wait_recv()
        pair = pl.ds(pair_of[g], 2)
        both = jnp.concatenate(
            [resident_agg[c, pair].reshape(rows, LANES) for c in range(2, chunks)], axis=1
        )
        total = jnp.dot(both, wg[pl.ds(2 * LANES, 2 * LANES)], preferred_element_type=F32)
        total = mixed[pair].reshape(rows, width) + total
        hid = resident_feat[pair].reshape(rows, width).astype(F32) + jnp.maximum(total, 0.0)
        hid = hid.astype(BF16)
        hidden[pair] = hid.reshape(2, tile, width)
        hid = hid.astype(F32)
        mean = jnp.mean(hid, axis=-1, keepdims=True)
        centred = hid - mean
        variance = jnp.mean(centred * centred, axis=-1, keepdims=True)
        normed = (centred * lax.rsqrt(variance + 1e-05) * gain[...]).astype(BF16)
        for i, to in enumerate((query, key, value)):
            product = jnp.dot(normed, wqkv[i], preferred_element_type=F32).astype(BF16).astype(F32)
            to[pair] = product.reshape(2, tile, width)

    def column(u):
        return pl.ds(u * LANES, LANES)

    def score_rows(i, carry):
        at = pl.ds(pl.multiple_of(i * 16, 16), 16)
        for t in range(snaps):
            for u in range(t + 1):
                total = query[t, at, column(0)] * key[u, at, column(0)]
                for v in range(1, chunks):
                    total = total + query[t, at, column(v)] * key[u, at, column(v)]
                partial[t, at, column(u)] = total.astype(BF16)
        return carry

    lax.fori_loop(0, tile // 16, score_rows, 0)

    for u in range(0, snaps, 2):
        at = pl.ds(u * LANES, 2 * LANES)
        later = (snaps - u) * tile
        summed = jnp.dot(
            partial[u:, :, at].reshape(later, 2 * LANES), head_sum[...], preferred_element_type=F32
        )
        scores[u:, :, at] = summed.reshape(snaps - u, tile, 2 * LANES)

    def context_rows(i, carry):
        at = pl.ds(pl.multiple_of(i * 16, 16), 16)
        for t in range(snaps):
            row = [scores[t, at, column(u)] for u in range(t + 1)]
            top = row[0]
            for x in row[1:]:
                top = jnp.maximum(top, x)
            row = [jnp.exp(x - top) for x in row]
            total = row[0]
            for x in row[1:]:
                total = total + x
            scale = 1.0 / total
            row = [(x * scale).astype(BF16).astype(F32) for x in row]
            for v in range(chunks):
                total = row[0] * value[0, at, column(v)]
                for u in range(1, t + 1):
                    total = total + row[u] * value[u, at, column(v)]
                context[t, at, column(v)] = total.astype(BF16)
        return carry

    lax.fori_loop(0, tile // 16, context_rows, 0)

    half = snaps // 2
    rows = half * tile
    for h in range(2):
        part_of = pl.ds(h * half, half)
        projected = jnp.dot(context[part_of].reshape(rows, width), wo[...], preferred_element_type=F32)
        result = hidden[part_of].astype(F32) + projected.reshape(half, tile, width)
        out[part_of] = result.astype(BF16)

    for c in range(chunks):
        for d in range(2):

            @pl.when(sends[d])
            def _():
                own(c, d).wait_send()

            @pl.when(has_both)
            def _():
                relay(c, d).wait_send()

        for p in peers:
            agg_with(c, p).wait_send()
    for p in peers:
        feat_with(p).wait_send()


def local_layer(
    snaps,
    ring,
    features,
    tile_rows,
    tile_cols,
    tile_values,
    tile_count,
    w_graph,
    norm_gain,
    w_query,
    w_key,
    w_value,
    w_out,
):
    nodes_dev, width = features.shape[1:]
    slots, tile = tile_values.shape[1:3]
    blocks = nodes_dev // tile
    chunks = width // LANES
    smem = pl.BlockSpec(memory_space=pltpu.SMEM)
    hbm = pl.BlockSpec(memory_space=pltpu.HBM)
    dma = pltpu.SemaphoreType.DMA

    def kernel(*refs):
        layer_kernel(snaps, ring, *refs)

    return pl.pallas_call(
        kernel,
        out_shape=pltpu.VMEM((snaps, tile, width), BF16),
        in_specs=[smem] * 3 + [hbm] * 8,
        out_specs=pl.BlockSpec(memory_space=pltpu.VMEM),
        scratch_shapes=[
            *[pltpu.VMEM((5 * blocks, tile, LANES), BF16)] * chunks,
            pltpu.VMEM((slots, tile, tile), BF16),
            pltpu.VMEM((slots + 1, tile, LANES), F32),
            pltpu.VMEM((chunks, blocks, tile, LANES), BF16),
            pltpu.VMEM((chunks, snaps, tile, LANES), BF16),
            pltpu.VMEM((snaps, tile, width), BF16),
            pltpu.VMEM((snaps, tile, width), F32),
            pltpu.VMEM((snaps, tile, width), BF16),
            pltpu.VMEM((snaps, tile, width), F32),
            pltpu.VMEM((snaps, tile, width), F32),
            pltpu.VMEM((snaps, tile, width), F32),
            pltpu.VMEM((width, width), BF16),
            pltpu.VMEM((1, width), F32),
            pltpu.VMEM((3, width, width), BF16),
            pltpu.VMEM((width, width), BF16),
            pltpu.VMEM((2 * LANES, 2 * LANES), BF16),
            pltpu.VMEM((snaps, tile, snaps * LANES), BF16),
            pltpu.VMEM((snaps, tile, snaps * LANES), F32),
            pltpu.VMEM((snaps, tile, width), BF16),
            *[pltpu.SMEM((slots,), jnp.int32)] * 4,
            pltpu.SMEM((slots,), F32),
            pltpu.SMEM((blocks,), jnp.int32),
            dma((2, chunks)),
            dma((2, chunks)),
            dma((2, chunks)),
            dma((2, chunks)),
            dma((snaps,)),
            dma((snaps,)),
            dma((chunks, snaps)),
            dma((chunks, snaps)),
            dma((8 + chunks,)),
        ],
        compiler_params=pltpu.CompilerParams(
            collective_id=0, has_side_effects=True, vmem_limit_bytes=58 * 2**20
        ),
        cost_estimate=pl.CostEstimate(
            flops=4 * 10**9, bytes_accessed=6 * 2**20, transcendentals=10**6
        ),
    )(
        tile_rows,
        tile_cols,
        tile_count,
        features.reshape(blocks, tile, width),
        tile_values[0],
        w_graph,
        norm_gain.reshape(1, width),
        w_query,
        w_key,
        w_value,
        w_out,
    )


def solution(mesh):
    snaps, ring = mesh.shape["snap"], mesh.shape["node"]

    def local(*args):
        return local_layer(snaps, ring, *args)

    in_specs = (
        P("snap", "node", None),
        P("snap", "node"),
        P("snap", "node"),
        P("snap", "node", None, None),
        P("snap", "node"),
        P(),
        P(),
        P(),
        P(),
        P(),
        P(),
    )
    return jax.shard_map(
        local, mesh=mesh, in_specs=in_specs, out_specs=P(None, ("node", "snap"), None), check_vma=False
    )
```

```python
import jax
import jax.numpy as jnp
from jax import lax
from jax.experimental import pallas as pl
from jax.experimental.pallas import tpu as pltpu
from jax.sharding import PartitionSpec as P

MESH = pl.DeviceIdType.MESH
HEADS = 8
HEAD_DIM = 64
LANES = 128
BF16 = jnp.bfloat16
F32 = jnp.float32


def layer_kernel(
    snaps,
    ring,
    rows_ref,
    cols_ref,
    count_ref,
    feat,
    tiles_hbm,
    wg_hbm,
    gain_hbm,
    wq_hbm,
    wk_hbm,
    wv_hbm,
    wo_hbm,
    out,
    win_a,
    win_b,
    win_c,
    win_d,
    win_e,
    last_columns,
    tiles,
    part,
    aggregated,
    resident_agg,
    aggregated_narrow,
    resident_narrow,
    resident_feat,
    mixed,
    hidden,
    query,
    key,
    value,
    wg,
    gain,
    wqkv,
    wo,
    head_sum,
    partial,
    scores,
    context,
    key_ref,
    rank_ref,
    slot_ref,
    column_ref,
    keep_ref,
    last_ref,
    own_send,
    own_recv,
    relay_send,
    relay_recv,
    feat_send,
    feat_recv,
    agg_send,
    agg_recv,
    local_sem,
):
    win = (win_a, win_b, win_c, win_d, win_e)
    blocks = feat.shape[0]
    tile = feat.shape[1]
    width = feat.shape[2]
    chunks = width // LANES
    narrow = LANES // 2
    sent = chunks + 1
    group = LANES // HEADS
    slots = tiles.shape[0]
    s = lax.axis_index("snap")
    j = lax.axis_index("node")
    right = lax.rem(j + 1, ring)
    left = lax.rem(j + ring - 1, ring)
    node_peer = (right, left)
    has_left, has_right = j > 0, j < ring - 1
    has_both = has_left & has_right
    sends, receives = (has_right, has_left), (has_left, has_right)
    receives_far = (j > 1, j < ring - 2)
    near = (blocks, 3 * blocks)
    far = (0, 4 * blocks)

    def cols_of(c):
        return pl.ds(c * LANES, LANES)

    local = [pltpu.make_async_copy(tiles_hbm, tiles, local_sem.at[0])]
    for c in range(chunks):
        place = last_columns if c == chunks - 1 else win[c].at[pl.ds(2 * blocks, blocks)]
        local.append(pltpu.make_async_copy(feat.at[:, :, cols_of(c)], place, local_sem.at[1 + c]))
    base = 1 + chunks
    weights = [
        pltpu.make_async_copy(wg_hbm, wg, local_sem.at[base]),
        pltpu.make_async_copy(gain_hbm, gain, local_sem.at[base + 1]),
        pltpu.make_async_copy(wq_hbm, wqkv.at[0], local_sem.at[base + 2]),
        pltpu.make_async_copy(wk_hbm, wqkv.at[1], local_sem.at[base + 3]),
        pltpu.make_async_copy(wv_hbm, wqkv.at[2], local_sem.at[base + 4]),
        pltpu.make_async_copy(wo_hbm, wo, local_sem.at[base + 5]),
        pltpu.make_async_copy(feat.at[s], resident_feat.at[s], local_sem.at[base + 6]),
    ]

    def own(c, d):
        return pltpu.make_async_remote_copy(
            src_ref=feat.at[:, :, cols_of(c)] if c < chunks - 1 else win[c].at[pl.ds(2 * blocks, blocks)],
            dst_ref=win[c].at[pl.ds(near[d], blocks)],
            send_sem=own_send.at[d, c],
            recv_sem=own_recv.at[d, c],
            device_id=(s, node_peer[d]),
            device_id_type=MESH,
        )

    def relay(c, d):
        return pltpu.make_async_remote_copy(
            src_ref=win[c].at[pl.ds(near[d], blocks)],
            dst_ref=win[c].at[pl.ds(far[d], blocks)],
            send_sem=relay_send.at[d, c],
            recv_sem=relay_recv.at[d, c],
            device_id=(s, node_peer[d]),
            device_id_type=MESH,
        )

    def feat_with(p):
        return pltpu.make_async_remote_copy(
            src_ref=feat.at[p],
            dst_ref=resident_feat.at[s],
            send_sem=feat_send.at[p],
            recv_sem=feat_recv.at[s],
            device_id=(p, j),
            device_id_type=MESH,
        )

    def feat_from(p):
        return pltpu.make_async_remote_copy(
            src_ref=feat.at[p],
            dst_ref=resident_feat.at[p],
            send_sem=feat_send.at[p],
            recv_sem=feat_recv.at[p],
            device_id=(p, j),
            device_id_type=MESH,
        )

    def agg_at(c, p):
        return aggregated.at[c, p] if c < chunks - 1 else aggregated_narrow.at[c - chunks + 1, p]

    def resident_at(c, p):
        return resident_agg.at[c, p] if c < chunks - 1 else resident_narrow.at[c - chunks + 1, p]

    def agg_with(c, p):
        return pltpu.make_async_remote_copy(
            src_ref=agg_at(c, p),
            dst_ref=resident_at(c, s),
            send_sem=agg_send.at[c, p],
            recv_sem=agg_recv.at[c, s],
            device_id=(p, j),
            device_id_type=MESH,
        )

    def agg_from(c, p):
        return pltpu.make_async_remote_copy(
            src_ref=agg_at(c, p),
            dst_ref=resident_at(c, p),
            send_sem=agg_send.at[c, p],
            recv_sem=agg_recv.at[c, p],
            device_id=(p, j),
            device_id_type=MESH,
        )

    chips = snaps // 2
    chip = lax.div(s, 2)
    other_core = s + 1 - 2 * lax.rem(s, 2)
    pair_of = [2 * lax.rem(chip + g, chips) for g in range(chips)]
    near_first = (0, 1, 3, 2)
    peers = [pair_of[g] + k for g in (2, 1, 3) for k in range(2)] + [other_core]

    barrier = pltpu.get_barrier_semaphore()
    for d in range(2):

        @pl.when(sends[d])
        def _():
            pl.semaphore_signal(barrier, inc=1, device_id=(s, node_peer[d]), device_id_type=MESH)

    for p in peers:
        pl.semaphore_signal(barrier, inc=1, device_id=(p, j), device_id_type=MESH)
    for copy in local:
        copy.start()
    for copy in weights:
        copy.start()
    pl.semaphore_wait(
        barrier, snaps - 1 + has_left.astype(jnp.int32) + has_right.astype(jnp.int32)
    )

    def start_own(c, d):
        @pl.when(sends[d])
        def _():
            own(c, d).start()

    for c in range(2):
        for d in range(2):
            start_own(c, d)
    for p in peers:
        feat_with(p).start()

    for copy in local:
        copy.wait()

    def lanes_swapped(x):
        return pltpu.roll(x.astype(F32), narrow, x.ndim - 1)

    def in_left_lanes(shape):
        return lax.broadcasted_iota(jnp.int32, shape, len(shape) - 1) < narrow

    for b in range(blocks):
        upper = last_columns[b, :narrow].astype(F32)
        lower = last_columns[b, narrow:].astype(F32)
        left = in_left_lanes(upper.shape)
        win_d[2 * blocks + b] = jnp.where(left, upper, lanes_swapped(lower)).astype(BF16)
        win_e[2 * blocks + b] = jnp.where(left, lanes_swapped(upper), lower).astype(BF16)

    live_slots = count_ref[0, 0]

    def find_key(t, carry):
        key_ref[t] = jnp.where(t < live_slots, rows_ref[0, t] - j * blocks, blocks)
        return carry

    def find_rank(t, carry):
        mine = key_ref[t]
        rank = jnp.int32(0)
        for o in range(slots):
            theirs = key_ref[o]
            ahead = (theirs < mine) | ((theirs == mine) & (o < t))
            rank = rank + ahead.astype(jnp.int32)
        rank_ref[t] = rank
        return carry

    def find_slot(p, last):
        slot = jnp.int32(0)
        for o in range(slots):
            slot = jnp.where(rank_ref[o] == p, o, slot)
        slot_ref[p] = slot
        row = key_ref[slot]
        column_ref[p] = jnp.clip(cols_ref[0, slot] - (j - 2) * blocks, 0, 5 * blocks - 1)
        keep_ref[p] = jnp.where(row == last[blocks], 1.0, 0.0)
        ends = tuple(jnp.where(row == r, p + 1, last[r]) for r in range(blocks))
        return ends + (row,)

    lax.fori_loop(0, slots, find_key, 0)
    lax.fori_loop(0, slots, find_rank, 0)
    last = lax.fori_loop(0, slots, find_slot, (jnp.int32(0),) * blocks + (jnp.int32(-1),))
    for r in range(blocks):
        last_ref[r] = last[r]

    place = lax.broadcasted_iota(jnp.int32, (width, width), 1)
    source = lax.broadcasted_iota(jnp.int32, (width, width), 0)
    moved = lax.rem(place, HEADS) * HEAD_DIM + place // LANES * group + lax.rem(place, LANES) // HEADS
    order = jnp.where(source == moved, 1.0, 0.0).astype(BF16)
    moved = lax.rem(source, HEADS) * HEAD_DIM + source // LANES * group + lax.rem(source, LANES) // HEADS
    order_back = jnp.where(place == moved, 1.0, 0.0).astype(BF16)
    lane = lax.broadcasted_iota(jnp.int32, (2 * LANES, 2 * LANES), 1)
    row = lax.broadcasted_iota(jnp.int32, (2 * LANES, 2 * LANES), 0)
    hit = (lane // LANES == row // LANES) & (lax.rem(lane, HEADS) == lax.rem(row, HEADS))
    head_sum[...] = jnp.where(hit, HEAD_DIM**-0.5, 0.0).astype(BF16)
    partial[...] = jnp.zeros(partial.shape, BF16)
    for copy in weights:
        copy.wait()
    for i in range(3):
        wqkv[i] = jnp.dot(wqkv[i], order, preferred_element_type=F32).astype(BF16)
    wo[...] = jnp.dot(order_back, wo[...], preferred_element_type=F32).astype(BF16)
    part[0] = jnp.zeros((tile, LANES), F32)

    unroll = 14

    def aggregate(c):
        def product(p, total):
            source = win[c][column_ref[p]]
            if c >= chunks - 1:
                source = jnp.concatenate([source, lanes_swapped(source).astype(BF16)], axis=0)
            term = jnp.dot(tiles[slot_ref[p]], source, preferred_element_type=F32)
            total = total * keep_ref[p] + term
            part[p + 1] = total
            return total

        def step(i, total):
            for k in range(unroll):
                total = product(i * unroll + k, total)
            return total

        total = lax.fori_loop(0, slots // unroll, step, jnp.zeros((tile, LANES), F32))
        for p in range(slots // unroll * unroll, slots):
            total = product(p, total)
        for r in range(blocks):
            total = part[last_ref[r]]
            if c < chunks - 1:
                aggregated[c, r] = total.astype(BF16)
            else:
                upper, lower = total[:narrow], lanes_swapped(total[narrow:])
                packed = jnp.where(in_left_lanes(upper.shape), upper, lower)
                aggregated_narrow[c - chunks + 1, r] = packed.astype(BF16)
        for p in peers:
            agg_with(c, p).start()
        if c < chunks - 1:
            resident_agg[c, s] = aggregated[c, s]
        else:
            resident_narrow[c - chunks + 1, s] = aggregated_narrow[c - chunks + 1, s]

    def pass_on(c):
        for d in range(2):

            @pl.when(receives[d])
            def _():
                own(c, d).wait_recv()

            @pl.when(has_both)
            def _():
                relay(c, d).start()

            if c + 2 < sent:
                start_own(c + 2, d)

    def arrived(c):
        for d in range(2):

            @pl.when(receives_far[d])
            def _():
                relay(c, d).wait_recv()

    def own_sent(c):
        for d in range(2):

            @pl.when(sends[d])
            def _():
                own(c, d).wait_send()

    def relay_sent(c):
        for d in range(2):

            @pl.when(has_both)
            def _():
                relay(c, d).wait_send()

    def agg_sent(c):
        for p in peers:
            agg_with(c, p).wait_send()

    pass_on(0)
    pass_on(1)
    for c in range(sent):
        arrived(c)
        aggregate(c)
        if c + 2 < sent:
            pass_on(c + 2)
        if c == 2:
            for c2 in range(2):
                for p in peers:
                    agg_from(c2, p).wait_recv()
            for u in range(snaps):
                both = jnp.concatenate([resident_agg[0, u], resident_agg[1, u]], axis=1)
                mixed[u] = jnp.dot(both, wg[pl.ds(0, 2 * LANES)], preferred_element_type=F32)
            for p in peers:
                feat_from(p).wait_recv()
            for p in peers:
                feat_with(p).wait_send()
            for c2 in range(2):
                relay_sent(c2)
                agg_sent(c2)
            for c2 in range(sent - 1):
                own_sent(c2)

    own_sent(sent - 1)
    relay_sent(2)
    agg_sent(2)
    rows = 2 * tile
    for g in near_first:
        for p in [other_core] if g == 0 else [pair_of[g], pair_of[g] + 1]:
            for c in range(2, sent):
                agg_from(c, p).wait_recv()
        pair = pl.ds(pair_of[g], 2)
        first, second = resident_narrow[0, pair].astype(F32), resident_narrow[1, pair].astype(F32)
        left = in_left_lanes(first.shape)
        upper = jnp.where(left, first, lanes_swapped(second))
        lower = jnp.where(left, lanes_swapped(first), second)
        joined = jnp.concatenate([upper, lower], axis=1).astype(BF16)
        both = jnp.concatenate(
            [resident_agg[2, pair].reshape(rows, LANES), joined.reshape(rows, LANES)], axis=1
        )
        total = jnp.dot(both, wg[pl.ds(2 * LANES, 2 * LANES)], preferred_element_type=F32)
        total = mixed[pair].reshape(rows, width) + total
        hid = resident_feat[pair].reshape(rows, width).astype(F32) + jnp.maximum(total, 0.0)
        hid = hid.astype(BF16)
        hidden[pair] = hid.reshape(2, tile, width)
        hid = hid.astype(F32)
        mean = jnp.mean(hid, axis=-1, keepdims=True)
        centred = hid - mean
        variance = jnp.mean(centred * centred, axis=-1, keepdims=True)
        normed = (centred * lax.rsqrt(variance + 1e-05) * gain[...]).astype(BF16)
        for i, to in enumerate((query, key, value)):
            product = jnp.dot(normed, wqkv[i], preferred_element_type=F32).astype(BF16).astype(F32)
            to[pair] = product.reshape(2, tile, width)

    def column(u):
        return pl.ds(u * LANES, LANES)

    def score_rows(i, carry):
        at = pl.ds(pl.multiple_of(i * 16, 16), 16)
        for t in range(snaps):
            for u in range(t + 1):
                total = query[t, at, column(0)] * key[u, at, column(0)]
                for v in range(1, chunks):
                    total = total + query[t, at, column(v)] * key[u, at, column(v)]
                partial[t, at, column(u)] = total.astype(BF16)
        return carry

    lax.fori_loop(0, tile // 16, score_rows, 0)

    for u in range(0, snaps, 2):
        at = pl.ds(u * LANES, 2 * LANES)
        later = (snaps - u) * tile
        summed = jnp.dot(
            partial[u:, :, at].reshape(later, 2 * LANES), head_sum[...], preferred_element_type=F32
        )
        scores[u:, :, at] = summed.reshape(snaps - u, tile, 2 * LANES)

    def context_rows(i, carry):
        at = pl.ds(pl.multiple_of(i * 16, 16), 16)
        for t in range(snaps):
            row = [scores[t, at, column(u)] for u in range(t + 1)]
            top = row[0]
            for x in row[1:]:
                top = jnp.maximum(top, x)
            row = [jnp.exp(x - top) for x in row]
            total = row[0]
            for x in row[1:]:
                total = total + x
            scale = 1.0 / total
            row = [(x * scale).astype(BF16).astype(F32) for x in row]
            for v in range(chunks):
                total = row[0] * value[0, at, column(v)]
                for u in range(1, t + 1):
                    total = total + row[u] * value[u, at, column(v)]
                context[t, at, column(v)] = total.astype(BF16)
        return carry

    lax.fori_loop(0, tile // 16, context_rows, 0)

    half = snaps // 2
    rows = half * tile
    for h in range(2):
        part_of = pl.ds(h * half, half)
        projected = jnp.dot(context[part_of].reshape(rows, width), wo[...], preferred_element_type=F32)
        result = hidden[part_of].astype(F32) + projected.reshape(half, tile, width)
        out[part_of] = result.astype(BF16)

    for c in range(3, sent):
        relay_sent(c)
        agg_sent(c)


def local_layer(
    snaps,
    ring,
    features,
    tile_rows,
    tile_cols,
    tile_values,
    tile_count,
    w_graph,
    norm_gain,
    w_query,
    w_key,
    w_value,
    w_out,
):
    nodes_dev, width = features.shape[1:]
    slots, tile = tile_values.shape[1:3]
    blocks = nodes_dev // tile
    chunks = width // LANES
    smem = pl.BlockSpec(memory_space=pltpu.SMEM)
    hbm = pl.BlockSpec(memory_space=pltpu.HBM)
    dma = pltpu.SemaphoreType.DMA

    def kernel(*refs):
        layer_kernel(snaps, ring, *refs)

    return pl.pallas_call(
        kernel,
        out_shape=pltpu.VMEM((snaps, tile, width), BF16),
        in_specs=[smem] * 3 + [hbm] * 8,
        out_specs=pl.BlockSpec(memory_space=pltpu.VMEM),
        scratch_shapes=[
            *[pltpu.VMEM((5 * blocks, tile, LANES), BF16)] * (chunks - 1),
            *[pltpu.VMEM((5 * blocks, tile // 2, LANES), BF16)] * 2,
            pltpu.VMEM((blocks, tile, LANES), BF16),
            pltpu.VMEM((slots, tile, tile), BF16),
            pltpu.VMEM((slots + 1, tile, LANES), F32),
            pltpu.VMEM((chunks - 1, blocks, tile, LANES), BF16),
            pltpu.VMEM((chunks - 1, snaps, tile, LANES), BF16),
            pltpu.VMEM((2, blocks, tile // 2, LANES), BF16),
            pltpu.VMEM((2, snaps, tile // 2, LANES), BF16),
            pltpu.VMEM((snaps, tile, width), BF16),
            pltpu.VMEM((snaps, tile, width), F32),
            pltpu.VMEM((snaps, tile, width), BF16),
            pltpu.VMEM((snaps, tile, width), F32),
            pltpu.VMEM((snaps, tile, width), F32),
            pltpu.VMEM((snaps, tile, width), F32),
            pltpu.VMEM((width, width), BF16),
            pltpu.VMEM((1, width), F32),
            pltpu.VMEM((3, width, width), BF16),
            pltpu.VMEM((width, width), BF16),
            pltpu.VMEM((2 * LANES, 2 * LANES), BF16),
            pltpu.VMEM((snaps, tile, snaps * LANES), BF16),
            pltpu.VMEM((snaps, tile, snaps * LANES), F32),
            pltpu.VMEM((snaps, tile, width), BF16),
            *[pltpu.SMEM((slots,), jnp.int32)] * 4,
            pltpu.SMEM((slots,), F32),
            pltpu.SMEM((blocks,), jnp.int32),
            dma((2, chunks + 1)),
            dma((2, chunks + 1)),
            dma((2, chunks + 1)),
            dma((2, chunks + 1)),
            dma((snaps,)),
            dma((snaps,)),
            dma((chunks + 1, snaps)),
            dma((chunks + 1, snaps)),
            dma((8 + chunks,)),
        ],
        compiler_params=pltpu.CompilerParams(
            collective_id=0, has_side_effects=True, vmem_limit_bytes=58 * 2**20
        ),
        cost_estimate=pl.CostEstimate(
            flops=4 * 10**9, bytes_accessed=6 * 2**20, transcendentals=10**6
        ),
    )(
        tile_rows,
        tile_cols,
        tile_count,
        features.reshape(blocks, tile, width),
        tile_values[0],
        w_graph,
        norm_gain.reshape(1, width),
        w_query,
        w_key,
        w_value,
        w_out,
    )


def solution(mesh):
    snaps, ring = mesh.shape["snap"], mesh.shape["node"]

    def local(*args):
        return local_layer(snaps, ring, *args)

    in_specs = (
        P("snap", "node", None),
        P("snap", "node"),
        P("snap", "node"),
        P("snap", "node", None, None),
        P("snap", "node"),
        P(),
        P(),
        P(),
        P(),
        P(),
        P(),
    )
    return jax.shard_map(
        local, mesh=mesh, in_specs=in_specs, out_specs=P(None, ("node", "snap"), None), check_vma=False
    )
```

```python
import jax
import jax.numpy as jnp
from jax import lax
from jax.experimental import pallas as pl
from jax.experimental.pallas import tpu as pltpu
from jax.sharding import PartitionSpec as P

MESH = pl.DeviceIdType.MESH
HEADS = 8
HEAD_DIM = 64
LANES = 128
BF16 = jnp.bfloat16
F32 = jnp.float32


def layer_kernel(
    snaps,
    ring,
    rows_ref,
    cols_ref,
    count_ref,
    feat,
    tiles_hbm,
    wg_hbm,
    gain_hbm,
    wq_hbm,
    wk_hbm,
    wv_hbm,
    wo_hbm,
    out,
    win_a,
    win_b,
    win_c,
    win_d,
    win_e,
    last_columns,
    tiles,
    part,
    aggregated,
    resident_agg,
    aggregated_narrow,
    resident_narrow,
    resident_feat,
    mixed,
    hidden,
    query,
    key,
    value,
    wg,
    gain,
    wqkv,
    wo,
    head_sum,
    partial,
    scores,
    context,
    key_ref,
    rank_ref,
    slot_ref,
    column_ref,
    keep_ref,
    last_ref,
    own_send,
    own_recv,
    relay_send,
    relay_recv,
    feat_send,
    feat_recv,
    agg_send,
    agg_recv,
    local_sem,
):
    win = (win_a, win_b, win_c, win_d, win_e)
    blocks = feat.shape[0]
    tile = feat.shape[1]
    width = feat.shape[2]
    chunks = width // LANES
    narrow = LANES // 2
    sent = chunks + 1
    group = LANES // HEADS
    slots = tiles.shape[0]
    s = lax.axis_index("snap")
    j = lax.axis_index("node")
    right = lax.rem(j + 1, ring)
    left = lax.rem(j + ring - 1, ring)
    node_peer = (right, left)
    has_left, has_right = j > 0, j < ring - 1
    has_both = has_left & has_right
    sends, receives = (has_right, has_left), (has_left, has_right)
    receives_far = (j > 1, j < ring - 2)
    near = (blocks, 3 * blocks)
    far = (0, 4 * blocks)

    def cols_of(c):
        return pl.ds(c * LANES, LANES)

    local = [pltpu.make_async_copy(tiles_hbm, tiles, local_sem.at[0])]
    for c in range(chunks):
        place = last_columns if c == chunks - 1 else win[c].at[pl.ds(2 * blocks, blocks)]
        local.append(pltpu.make_async_copy(feat.at[:, :, cols_of(c)], place, local_sem.at[1 + c]))
    base = 1 + chunks
    weights = [
        pltpu.make_async_copy(wg_hbm, wg, local_sem.at[base]),
        pltpu.make_async_copy(gain_hbm, gain, local_sem.at[base + 1]),
        pltpu.make_async_copy(wq_hbm, wqkv.at[0], local_sem.at[base + 2]),
        pltpu.make_async_copy(wk_hbm, wqkv.at[1], local_sem.at[base + 3]),
        pltpu.make_async_copy(wv_hbm, wqkv.at[2], local_sem.at[base + 4]),
        pltpu.make_async_copy(wo_hbm, wo, local_sem.at[base + 5]),
        pltpu.make_async_copy(feat.at[s], resident_feat.at[s], local_sem.at[base + 6]),
    ]

    def own(c, d):
        return pltpu.make_async_remote_copy(
            src_ref=feat.at[:, :, cols_of(c)] if c < chunks - 1 else win[c].at[pl.ds(2 * blocks, blocks)],
            dst_ref=win[c].at[pl.ds(near[d], blocks)],
            send_sem=own_send.at[d, c],
            recv_sem=own_recv.at[d, c],
            device_id=(s, node_peer[d]),
            device_id_type=MESH,
        )

    def relay(c, d):
        return pltpu.make_async_remote_copy(
            src_ref=win[c].at[pl.ds(near[d], blocks)],
            dst_ref=win[c].at[pl.ds(far[d], blocks)],
            send_sem=relay_send.at[d, c],
            recv_sem=relay_recv.at[d, c],
            device_id=(s, node_peer[d]),
            device_id_type=MESH,
        )

    def feat_with(p):
        return pltpu.make_async_remote_copy(
            src_ref=feat.at[p],
            dst_ref=resident_feat.at[s],
            send_sem=feat_send.at[p],
            recv_sem=feat_recv.at[s],
            device_id=(p, j),
            device_id_type=MESH,
        )

    def feat_from(p):
        return pltpu.make_async_remote_copy(
            src_ref=feat.at[p],
            dst_ref=resident_feat.at[p],
            send_sem=feat_send.at[p],
            recv_sem=feat_recv.at[p],
            device_id=(p, j),
            device_id_type=MESH,
        )

    def agg_at(c, p):
        return aggregated.at[c, p] if c < chunks - 1 else aggregated_narrow.at[c - chunks + 1, p]

    def resident_at(c, p):
        return resident_agg.at[c, p] if c < chunks - 1 else resident_narrow.at[c - chunks + 1, p]

    def agg_with(c, p):
        return pltpu.make_async_remote_copy(
            src_ref=agg_at(c, p),
            dst_ref=resident_at(c, s),
            send_sem=agg_send.at[c, p],
            recv_sem=agg_recv.at[c, s],
            device_id=(p, j),
            device_id_type=MESH,
        )

    def agg_from(c, p):
        return pltpu.make_async_remote_copy(
            src_ref=agg_at(c, p),
            dst_ref=resident_at(c, p),
            send_sem=agg_send.at[c, p],
            recv_sem=agg_recv.at[c, p],
            device_id=(p, j),
            device_id_type=MESH,
        )

    chips = snaps // 2
    chip = lax.div(s, 2)
    other_core = s + 1 - 2 * lax.rem(s, 2)
    pair_of = [2 * lax.rem(chip + g, chips) for g in range(chips)]
    near_first = (0, 1, 3, 2)
    peers = [pair_of[g] + k for g in (2, 1, 3) for k in range(2)] + [other_core]

    barrier = pltpu.get_barrier_semaphore()
    for d in range(2):

        @pl.when(sends[d])
        def _():
            pl.semaphore_signal(barrier, inc=1, device_id=(s, node_peer[d]), device_id_type=MESH)

    for p in peers:
        pl.semaphore_signal(barrier, inc=1, device_id=(p, j), device_id_type=MESH)
    for copy in local:
        copy.start()
    for copy in weights:
        copy.start()
    pl.semaphore_wait(
        barrier, snaps - 1 + has_left.astype(jnp.int32) + has_right.astype(jnp.int32)
    )

    def start_own(c, d):
        @pl.when(sends[d])
        def _():
            own(c, d).start()

    for c in range(2):
        for d in range(2):
            start_own(c, d)
    for p in peers:
        feat_with(p).start()

    for copy in local:
        copy.wait()

    def lanes_swapped(x):
        return pltpu.roll(x.astype(F32), narrow, x.ndim - 1)

    def in_left_lanes(shape):
        return lax.broadcasted_iota(jnp.int32, shape, len(shape) - 1) < narrow

    for b in range(blocks):
        upper = last_columns[b, :narrow].astype(F32)
        lower = last_columns[b, narrow:].astype(F32)
        left = in_left_lanes(upper.shape)
        win_d[2 * blocks + b] = jnp.where(left, upper, lanes_swapped(lower)).astype(BF16)
        win_e[2 * blocks + b] = jnp.where(left, lanes_swapped(upper), lower).astype(BF16)

    live_slots = count_ref[0, 0]

    def find_key(t, carry):
        key_ref[t] = jnp.where(t < live_slots, rows_ref[0, t] - j * blocks, blocks)
        return carry

    def find_rank(t, carry):
        mine = key_ref[t]
        rank = jnp.int32(0)
        for o in range(slots):
            theirs = key_ref[o]
            ahead = (theirs < mine) | ((theirs == mine) & (o < t))
            rank = rank + ahead.astype(jnp.int32)
        rank_ref[t] = rank
        return carry

    def find_slot(p, last):
        slot = jnp.int32(0)
        for o in range(slots):
            slot = jnp.where(rank_ref[o] == p, o, slot)
        slot_ref[p] = slot
        row = key_ref[slot]
        column_ref[p] = jnp.clip(cols_ref[0, slot] - (j - 2) * blocks, 0, 5 * blocks - 1)
        keep_ref[p] = jnp.where(row == last[blocks], 1.0, 0.0)
        ends = tuple(jnp.where(row == r, p + 1, last[r]) for r in range(blocks))
        return ends + (row,)

    lax.fori_loop(0, slots, find_key, 0)
    lax.fori_loop(0, slots, find_rank, 0)
    last = lax.fori_loop(0, slots, find_slot, (jnp.int32(0),) * blocks + (jnp.int32(-1),))
    for r in range(blocks):
        last_ref[r] = last[r]

    place = lax.broadcasted_iota(jnp.int32, (width, width), 1)
    source = lax.broadcasted_iota(jnp.int32, (width, width), 0)
    moved = lax.rem(place, HEADS) * HEAD_DIM + place // LANES * group + lax.rem(place, LANES) // HEADS
    order = jnp.where(source == moved, 1.0, 0.0).astype(BF16)
    moved = lax.rem(source, HEADS) * HEAD_DIM + source // LANES * group + lax.rem(source, LANES) // HEADS
    order_back = jnp.where(place == moved, 1.0, 0.0).astype(BF16)
    lane = lax.broadcasted_iota(jnp.int32, (2 * LANES, 2 * LANES), 1)
    row = lax.broadcasted_iota(jnp.int32, (2 * LANES, 2 * LANES), 0)
    hit = (lane // LANES == row // LANES) & (lax.rem(lane, HEADS) == lax.rem(row, HEADS))
    head_sum[...] = jnp.where(hit, HEAD_DIM**-0.5, 0.0).astype(BF16)
    partial[...] = jnp.zeros(partial.shape, BF16)
    for copy in weights:
        copy.wait()
    for i in range(3):
        wqkv[i] = jnp.dot(wqkv[i], order, preferred_element_type=F32).astype(BF16)
    wo[...] = jnp.dot(order_back, wo[...], preferred_element_type=F32).astype(BF16)
    part[0] = jnp.zeros((tile, LANES), F32)

    unroll = 14

    def aggregate(c):
        def product(p, total):
            source = win[c][column_ref[p]]
            if c >= chunks - 1:
                source = jnp.concatenate([source, lanes_swapped(source).astype(BF16)], axis=0)
            term = jnp.dot(tiles[slot_ref[p]], source, preferred_element_type=F32)
            total = total * keep_ref[p] + term
            part[p + 1] = total
            return total

        def step(i, total):
            for k in range(unroll):
                total = product(i * unroll + k, total)
            return total

        total = lax.fori_loop(0, slots // unroll, step, jnp.zeros((tile, LANES), F32))
        for p in range(slots // unroll * unroll, slots):
            total = product(p, total)
        for r in range(blocks):
            total = part[last_ref[r]]
            if c < chunks - 1:
                aggregated[c, r] = total.astype(BF16)
            else:
                upper, lower = total[:narrow], lanes_swapped(total[narrow:])
                packed = jnp.where(in_left_lanes(upper.shape), upper, lower)
                aggregated_narrow[c - chunks + 1, r] = packed.astype(BF16)
        for p in peers:
            agg_with(c, p).start()
        if c < chunks - 1:
            resident_agg[c, s] = aggregated[c, s]
        else:
            resident_narrow[c - chunks + 1, s] = aggregated_narrow[c - chunks + 1, s]

    def pass_on(c):
        for d in range(2):

            @pl.when(receives[d])
            def _():
                own(c, d).wait_recv()

            @pl.when(has_both)
            def _():
                relay(c, d).start()

            if c + 2 < sent:
                start_own(c + 2, d)

    def arrived(c):
        for d in range(2):

            @pl.when(receives_far[d])
            def _():
                relay(c, d).wait_recv()

    def own_sent(c):
        for d in range(2):

            @pl.when(sends[d])
            def _():
                own(c, d).wait_send()

    def relay_sent(c):
        for d in range(2):

            @pl.when(has_both)
            def _():
                relay(c, d).wait_send()

    def agg_sent(c):
        for p in peers:
            agg_with(c, p).wait_send()

    pass_on(0)
    pass_on(1)
    for c in range(sent):
        arrived(c)
        aggregate(c)
        if c + 2 < sent:
            pass_on(c + 2)
        if c == 2:
            for c2 in range(2):
                for p in peers:
                    agg_from(c2, p).wait_recv()
            for u in range(snaps):
                both = jnp.concatenate([resident_agg[0, u], resident_agg[1, u]], axis=1)
                mixed[u] = jnp.dot(both, wg[pl.ds(0, 2 * LANES)], preferred_element_type=F32)
            for p in peers:
                feat_from(p).wait_recv()
            for p in peers:
                feat_with(p).wait_send()
            for c2 in range(2):
                relay_sent(c2)
                agg_sent(c2)
            for c2 in range(sent - 1):
                own_sent(c2)

    own_sent(sent - 1)
    relay_sent(2)
    agg_sent(2)
    rows = 2 * tile
    for g in near_first:
        for p in [other_core] if g == 0 else [pair_of[g], pair_of[g] + 1]:
            for c in range(2, sent):
                agg_from(c, p).wait_recv()
        pair = pl.ds(pair_of[g], 2)
        first, second = resident_narrow[0, pair].astype(F32), resident_narrow[1, pair].astype(F32)
        left = in_left_lanes(first.shape)
        upper = jnp.where(left, first, lanes_swapped(second))
        lower = jnp.where(left, lanes_swapped(first), second)
        joined = jnp.concatenate([upper, lower], axis=1).astype(BF16)
        both = jnp.concatenate(
            [resident_agg[2, pair].reshape(rows, LANES), joined.reshape(rows, LANES)], axis=1
        )
        total = jnp.dot(both, wg[pl.ds(2 * LANES, 2 * LANES)], preferred_element_type=F32)
        total = mixed[pair].reshape(rows, width) + total
        hid = resident_feat[pair].reshape(rows, width).astype(F32) + jnp.maximum(total, 0.0)
        hid = hid.astype(BF16)
        hidden[pair] = hid.reshape(2, tile, width)
        hid = hid.astype(F32)
        mean = jnp.mean(hid, axis=-1, keepdims=True)
        centred = hid - mean
        variance = jnp.mean(centred * centred, axis=-1, keepdims=True)
        normed = (centred * lax.rsqrt(variance + 1e-05) * gain[...]).astype(BF16)
        for i, to in enumerate((query, key, value)):
            product = jnp.dot(normed, wqkv[i], preferred_element_type=F32)
            to[pair] = product.reshape(2, tile, width)

    def column(u):
        return pl.ds(u * LANES, LANES)

    def score_rows(i, carry):
        at = pl.ds(pl.multiple_of(i * 16, 16), 16)
        for t in range(snaps):
            for u in range(t + 1):
                total = query[t, at, column(0)] * key[u, at, column(0)]
                for v in range(1, chunks):
                    total = total + query[t, at, column(v)] * key[u, at, column(v)]
                partial[t, at, column(u)] = total.astype(BF16)
        return carry

    lax.fori_loop(0, tile // 32, lambda i, x: score_rows(2 * i + 1, score_rows(2 * i, x)), 0)

    for u in range(0, snaps, 2):
        at = pl.ds(u * LANES, 2 * LANES)
        later = (snaps - u) * tile
        summed = jnp.dot(
            partial[u:, :, at].reshape(later, 2 * LANES), head_sum[...], preferred_element_type=F32
        )
        scores[u:, :, at] = summed.reshape(snaps - u, tile, 2 * LANES)

    def context_rows(i, carry):
        at = pl.ds(pl.multiple_of(i * 16, 16), 16)
        for t in range(snaps):
            row = [scores[t, at, column(u)] for u in range(t + 1)]
            top = row[0]
            for x in row[1:]:
                top = jnp.maximum(top, x)
            row = [jnp.exp(x - top) for x in row]
            total = row[0]
            for x in row[1:]:
                total = total + x
            scale = 1.0 / total
            row = [x * scale for x in row]
            for v in range(chunks):
                total = row[0] * value[0, at, column(v)]
                for u in range(1, t + 1):
                    total = total + row[u] * value[u, at, column(v)]
                context[t, at, column(v)] = total.astype(BF16)
        return carry

    lax.fori_loop(0, tile // 32, lambda i, x: context_rows(2 * i + 1, context_rows(2 * i, x)), 0)

    half = snaps // 2
    rows = half * tile
    for h in range(2):
        part_of = pl.ds(h * half, half)
        projected = jnp.dot(context[part_of].reshape(rows, width), wo[...], preferred_element_type=F32)
        result = hidden[part_of].astype(F32) + projected.reshape(half, tile, width)
        out[part_of] = result.astype(BF16)

    for c in range(3, sent):
        relay_sent(c)
        agg_sent(c)


def local_layer(
    snaps,
    ring,
    features,
    tile_rows,
    tile_cols,
    tile_values,
    tile_count,
    w_graph,
    norm_gain,
    w_query,
    w_key,
    w_value,
    w_out,
):
    nodes_dev, width = features.shape[1:]
    slots, tile = tile_values.shape[1:3]
    blocks = nodes_dev // tile
    chunks = width // LANES
    smem = pl.BlockSpec(memory_space=pltpu.SMEM)
    hbm = pl.BlockSpec(memory_space=pltpu.HBM)
    dma = pltpu.SemaphoreType.DMA

    def kernel(*refs):
        layer_kernel(snaps, ring, *refs)

    return pl.pallas_call(
        kernel,
        out_shape=pltpu.VMEM((snaps, tile, width), BF16),
        in_specs=[smem] * 3 + [hbm] * 8,
        out_specs=pl.BlockSpec(memory_space=pltpu.VMEM),
        scratch_shapes=[
            *[pltpu.VMEM((5 * blocks, tile, LANES), BF16)] * (chunks - 1),
            *[pltpu.VMEM((5 * blocks, tile // 2, LANES), BF16)] * 2,
            pltpu.VMEM((blocks, tile, LANES), BF16),
            pltpu.VMEM((slots, tile, tile), BF16),
            pltpu.VMEM((slots + 1, tile, LANES), F32),
            pltpu.VMEM((chunks - 1, blocks, tile, LANES), BF16),
            pltpu.VMEM((chunks - 1, snaps, tile, LANES), BF16),
            pltpu.VMEM((2, blocks, tile // 2, LANES), BF16),
            pltpu.VMEM((2, snaps, tile // 2, LANES), BF16),
            pltpu.VMEM((snaps, tile, width), BF16),
            pltpu.VMEM((snaps, tile, width), F32),
            pltpu.VMEM((snaps, tile, width), BF16),
            pltpu.VMEM((snaps, tile, width), F32),
            pltpu.VMEM((snaps, tile, width), F32),
            pltpu.VMEM((snaps, tile, width), F32),
            pltpu.VMEM((width, width), BF16),
            pltpu.VMEM((1, width), F32),
            pltpu.VMEM((3, width, width), BF16),
            pltpu.VMEM((width, width), BF16),
            pltpu.VMEM((2 * LANES, 2 * LANES), BF16),
            pltpu.VMEM((snaps, tile, snaps * LANES), BF16),
            pltpu.VMEM((snaps, tile, snaps * LANES), F32),
            pltpu.VMEM((snaps, tile, width), BF16),
            *[pltpu.SMEM((slots,), jnp.int32)] * 4,
            pltpu.SMEM((slots,), F32),
            pltpu.SMEM((blocks,), jnp.int32),
            dma((2, chunks + 1)),
            dma((2, chunks + 1)),
            dma((2, chunks + 1)),
            dma((2, chunks + 1)),
            dma((snaps,)),
            dma((snaps,)),
            dma((chunks + 1, snaps)),
            dma((chunks + 1, snaps)),
            dma((8 + chunks,)),
        ],
        compiler_params=pltpu.CompilerParams(
            collective_id=0, has_side_effects=True, vmem_limit_bytes=58 * 2**20
        ),
        cost_estimate=pl.CostEstimate(
            flops=4 * 10**9, bytes_accessed=6 * 2**20, transcendentals=10**6
        ),
    )(
        tile_rows,
        tile_cols,
        tile_count,
        features.reshape(blocks, tile, width),
        tile_values[0],
        w_graph,
        norm_gain.reshape(1, width),
        w_query,
        w_key,
        w_value,
        w_out,
    )


def solution(mesh):
    snaps, ring = mesh.shape["snap"], mesh.shape["node"]

    def local(*args):
        return local_layer(snaps, ring, *args)

    in_specs = (
        P("snap", "node", None),
        P("snap", "node"),
        P("snap", "node"),
        P("snap", "node", None, None),
        P("snap", "node"),
        P(),
        P(),
        P(),
        P(),
        P(),
        P(),
    )
    return jax.shard_map(
        local, mesh=mesh, in_specs=in_specs, out_specs=P(None, ("node", "snap"), None), check_vma=False
    )
```

```python
import jax
import jax.numpy as jnp
from jax import lax
from jax.experimental import pallas as pl
from jax.experimental.pallas import tpu as pltpu
from jax.sharding import PartitionSpec as P

MESH = pl.DeviceIdType.MESH
HEADS = 8
HEAD_DIM = 64
LANES = 128
BF16 = jnp.bfloat16
F32 = jnp.float32


def layer_kernel(
    snaps,
    ring,
    rows_ref,
    cols_ref,
    count_ref,
    feat,
    tiles_hbm,
    wg_hbm,
    gain_hbm,
    wq_hbm,
    wk_hbm,
    wv_hbm,
    wo_hbm,
    out,
    win_a,
    win_b,
    win_c,
    win_d,
    win_e,
    last_columns,
    tiles,
    part,
    aggregated,
    resident_agg,
    aggregated_narrow,
    resident_narrow,
    resident_feat,
    mixed,
    hidden,
    query,
    key,
    value,
    wg,
    gain,
    wqkv,
    wo,
    head_sum,
    partial,
    scores,
    context,
    key_ref,
    rank_ref,
    slot_ref,
    column_ref,
    keep_ref,
    last_ref,
    own_send,
    own_recv,
    relay_send,
    relay_recv,
    feat_send,
    feat_recv,
    agg_send,
    agg_recv,
    local_sem,
):
    win = (win_a, win_b, win_c, win_d, win_e)
    blocks = feat.shape[0]
    tile = feat.shape[1]
    width = feat.shape[2]
    chunks = width // LANES
    narrow = LANES // 2
    sent = chunks + 1
    group = LANES // HEADS
    slots = tiles.shape[0]
    s = lax.axis_index("snap")
    j = lax.axis_index("node")
    right = lax.rem(j + 1, ring)
    left = lax.rem(j + ring - 1, ring)
    node_peer = (right, left)
    has_left, has_right = j > 0, j < ring - 1
    has_both = has_left & has_right
    sends, receives = (has_right, has_left), (has_left, has_right)
    receives_far = (j > 1, j < ring - 2)
    near = (blocks, 3 * blocks)
    far = (0, 4 * blocks)

    def cols_of(c):
        return pl.ds(c * LANES, LANES)

    local = [pltpu.make_async_copy(tiles_hbm, tiles, local_sem.at[0])]
    for c in range(chunks):
        place = last_columns if c == chunks - 1 else win[c].at[pl.ds(2 * blocks, blocks)]
        local.append(pltpu.make_async_copy(feat.at[:, :, cols_of(c)], place, local_sem.at[1 + c]))
    base = 1 + chunks
    weights = [
        pltpu.make_async_copy(wg_hbm, wg, local_sem.at[base]),
        pltpu.make_async_copy(gain_hbm, gain, local_sem.at[base + 1]),
        pltpu.make_async_copy(wq_hbm, wqkv.at[0], local_sem.at[base + 2]),
        pltpu.make_async_copy(wk_hbm, wqkv.at[1], local_sem.at[base + 3]),
        pltpu.make_async_copy(wv_hbm, wqkv.at[2], local_sem.at[base + 4]),
        pltpu.make_async_copy(wo_hbm, wo, local_sem.at[base + 5]),
        pltpu.make_async_copy(feat.at[s], resident_feat.at[s], local_sem.at[base + 6]),
    ]

    def own(c, d):
        return pltpu.make_async_remote_copy(
            src_ref=feat.at[:, :, cols_of(c)] if c < chunks - 1 else win[c].at[pl.ds(2 * blocks, blocks)],
            dst_ref=win[c].at[pl.ds(near[d], blocks)],
            send_sem=own_send.at[d, c],
            recv_sem=own_recv.at[d, c],
            device_id=(s, node_peer[d]),
            device_id_type=MESH,
        )

    def relay(c, d):
        return pltpu.make_async_remote_copy(
            src_ref=win[c].at[pl.ds(near[d], blocks)],
            dst_ref=win[c].at[pl.ds(far[d], blocks)],
            send_sem=relay_send.at[d, c],
            recv_sem=relay_recv.at[d, c],
            device_id=(s, node_peer[d]),
            device_id_type=MESH,
        )

    def feat_with(p):
        return pltpu.make_async_remote_copy(
            src_ref=feat.at[p],
            dst_ref=resident_feat.at[s],
            send_sem=feat_send.at[p],
            recv_sem=feat_recv.at[s],
            device_id=(p, j),
            device_id_type=MESH,
        )

    def feat_from(p):
        return pltpu.make_async_remote_copy(
            src_ref=feat.at[p],
            dst_ref=resident_feat.at[p],
            send_sem=feat_send.at[p],
            recv_sem=feat_recv.at[p],
            device_id=(p, j),
            device_id_type=MESH,
        )

    def agg_at(c, p):
        return aggregated.at[c, p] if c < chunks - 1 else aggregated_narrow.at[c - chunks + 1, p]

    def resident_at(c, p):
        return resident_agg.at[c, p] if c < chunks - 1 else resident_narrow.at[c - chunks + 1, p]

    def agg_with(c, p):
        return pltpu.make_async_remote_copy(
            src_ref=agg_at(c, p),
            dst_ref=resident_at(c, s),
            send_sem=agg_send.at[c, p],
            recv_sem=agg_recv.at[c, s],
            device_id=(p, j),
            device_id_type=MESH,
        )

    def agg_from(c, p):
        return pltpu.make_async_remote_copy(
            src_ref=agg_at(c, p),
            dst_ref=resident_at(c, p),
            send_sem=agg_send.at[c, p],
            recv_sem=agg_recv.at[c, p],
            device_id=(p, j),
            device_id_type=MESH,
        )

    chips = snaps // 2
    chip = lax.div(s, 2)
    other_core = s + 1 - 2 * lax.rem(s, 2)
    pair_of = [2 * lax.rem(chip + g, chips) for g in range(chips)]
    near_first = (0, 1, 3, 2)
    peers = [pair_of[g] + k for g in (2, 1, 3) for k in range(2)] + [other_core]

    barrier = pltpu.get_barrier_semaphore()
    for d in range(2):

        @pl.when(sends[d])
        def _():
            pl.semaphore_signal(barrier, inc=1, device_id=(s, node_peer[d]), device_id_type=MESH)

    for p in peers:
        pl.semaphore_signal(barrier, inc=1, device_id=(p, j), device_id_type=MESH)
    for copy in local:
        copy.start()
    for copy in weights:
        copy.start()
    pl.semaphore_wait(
        barrier, snaps - 1 + has_left.astype(jnp.int32) + has_right.astype(jnp.int32)
    )

    def start_own(c, d):
        @pl.when(sends[d])
        def _():
            own(c, d).start()

    for c in range(2):
        for d in range(2):
            start_own(c, d)
    for p in peers:
        feat_with(p).start()

    for copy in local:
        copy.wait()

    def lanes_swapped(x):
        return pltpu.roll(x.astype(F32), narrow, x.ndim - 1)

    def in_left_lanes(shape):
        return lax.broadcasted_iota(jnp.int32, shape, len(shape) - 1) < narrow

    for b in range(blocks):
        upper = last_columns[b, :narrow].astype(F32)
        lower = last_columns[b, narrow:].astype(F32)
        left = in_left_lanes(upper.shape)
        win_d[2 * blocks + b] = jnp.where(left, upper, lanes_swapped(lower)).astype(BF16)
        win_e[2 * blocks + b] = jnp.where(left, lanes_swapped(upper), lower).astype(BF16)

    live_slots = count_ref[0, 0]

    def find_key(t, carry):
        key_ref[t] = jnp.where(t < live_slots, rows_ref[0, t] - j * blocks, blocks)
        return carry

    def find_rank(t, carry):
        mine = key_ref[t]
        rank = jnp.int32(0)
        for o in range(slots):
            theirs = key_ref[o]
            ahead = (theirs < mine) | ((theirs == mine) & (o < t))
            rank = rank + ahead.astype(jnp.int32)
        rank_ref[t] = rank
        return carry

    def find_slot(p, last):
        slot = jnp.int32(0)
        for o in range(slots):
            slot = jnp.where(rank_ref[o] == p, o, slot)
        slot_ref[p] = slot
        row = key_ref[slot]
        column_ref[p] = jnp.clip(cols_ref[0, slot] - (j - 2) * blocks, 0, 5 * blocks - 1)
        keep_ref[p] = jnp.where(row == last[blocks], 1.0, 0.0)
        ends = tuple(jnp.where(row == r, p + 1, last[r]) for r in range(blocks))
        return ends + (row,)

    lax.fori_loop(0, slots, find_key, 0)
    lax.fori_loop(0, slots, find_rank, 0)
    last = lax.fori_loop(0, slots, find_slot, (jnp.int32(0),) * blocks + (jnp.int32(-1),))
    for r in range(blocks):
        last_ref[r] = last[r]

    place = lax.broadcasted_iota(jnp.int32, (width, width), 1)
    source = lax.broadcasted_iota(jnp.int32, (width, width), 0)
    moved = lax.rem(place, HEADS) * HEAD_DIM + place // LANES * group + lax.rem(place, LANES) // HEADS
    order = jnp.where(source == moved, 1.0, 0.0).astype(BF16)
    moved = lax.rem(source, HEADS) * HEAD_DIM + source // LANES * group + lax.rem(source, LANES) // HEADS
    order_back = jnp.where(place == moved, 1.0, 0.0).astype(BF16)
    lane = lax.broadcasted_iota(jnp.int32, (2 * LANES, 2 * LANES), 1)
    row = lax.broadcasted_iota(jnp.int32, (2 * LANES, 2 * LANES), 0)
    hit = (lane // LANES == row // LANES) & (lax.rem(lane, HEADS) == lax.rem(row, HEADS))
    head_sum[...] = jnp.where(hit, HEAD_DIM**-0.5, 0.0).astype(BF16)
    partial[...] = jnp.zeros(partial.shape, BF16)
    for copy in weights:
        copy.wait()
    for i in range(3):
        wqkv[i] = jnp.dot(wqkv[i], order, preferred_element_type=F32).astype(BF16)
    wo[...] = jnp.dot(order_back, wo[...], preferred_element_type=F32).astype(BF16)
    part[0] = jnp.zeros((tile, LANES), F32)

    unroll = 28

    def aggregate(c):
        def product(p, total):
            source = win[c][column_ref[p]]
            if c >= chunks - 1:
                source = jnp.concatenate([source, lanes_swapped(source).astype(BF16)], axis=0)
            term = jnp.dot(tiles[slot_ref[p]], source, preferred_element_type=F32)
            total = total * keep_ref[p] + term
            part[p + 1] = total
            return total

        def step(i, total):
            for k in range(unroll):
                total = product(i * unroll + k, total)
            return total

        total = lax.fori_loop(0, slots // unroll, step, jnp.zeros((tile, LANES), F32))
        for p in range(slots // unroll * unroll, slots):
            total = product(p, total)
        for r in range(blocks):
            total = part[last_ref[r]]
            if c < chunks - 1:
                aggregated[c, r] = total.astype(BF16)
            else:
                upper, lower = total[:narrow], lanes_swapped(total[narrow:])
                packed = jnp.where(in_left_lanes(upper.shape), upper, lower)
                aggregated_narrow[c - chunks + 1, r] = packed.astype(BF16)
        for p in peers:
            agg_with(c, p).start()
        if c < chunks - 1:
            resident_agg[c, s] = aggregated[c, s]
        else:
            resident_narrow[c - chunks + 1, s] = aggregated_narrow[c - chunks + 1, s]

    def pass_on(c):
        for d in range(2):

            @pl.when(receives[d])
            def _():
                own(c, d).wait_recv()

            @pl.when(has_both)
            def _():
                relay(c, d).start()

            if c + 2 < sent:
                start_own(c + 2, d)

    def arrived(c):
        for d in range(2):

            @pl.when(receives_far[d])
            def _():
                relay(c, d).wait_recv()

    def own_sent(c):
        for d in range(2):

            @pl.when(sends[d])
            def _():
                own(c, d).wait_send()

    def relay_sent(c):
        for d in range(2):

            @pl.when(has_both)
            def _():
                relay(c, d).wait_send()

    def agg_sent(c):
        for p in peers:
            agg_with(c, p).wait_send()

    pass_on(0)
    pass_on(1)
    for c in range(sent):
        arrived(c)
        aggregate(c)
        if c + 2 < sent:
            pass_on(c + 2)
        if c == 2:
            for c2 in range(2):
                for p in peers:
                    agg_from(c2, p).wait_recv()
            for u in range(snaps):
                both = jnp.concatenate([resident_agg[0, u], resident_agg[1, u]], axis=1)
                mixed[u] = jnp.dot(both, wg[pl.ds(0, 2 * LANES)], preferred_element_type=F32)
            for p in peers:
                feat_from(p).wait_recv()
            for p in peers:
                feat_with(p).wait_send()
            for c2 in range(2):
                relay_sent(c2)
                agg_sent(c2)
            for c2 in range(sent - 1):
                own_sent(c2)

    own_sent(sent - 1)
    relay_sent(2)
    agg_sent(2)
    rows = 2 * tile
    for g in near_first:
        for p in [other_core] if g == 0 else [pair_of[g], pair_of[g] + 1]:
            for c in range(2, sent):
                agg_from(c, p).wait_recv()
        pair = pl.ds(pair_of[g], 2)
        first, second = resident_narrow[0, pair].astype(F32), resident_narrow[1, pair].astype(F32)
        left = in_left_lanes(first.shape)
        upper = jnp.where(left, first, lanes_swapped(second))
        lower = jnp.where(left, lanes_swapped(first), second)
        joined = jnp.concatenate([upper, lower], axis=1).astype(BF16)
        both = jnp.concatenate(
            [resident_agg[2, pair].reshape(rows, LANES), joined.reshape(rows, LANES)], axis=1
        )
        total = jnp.dot(both, wg[pl.ds(2 * LANES, 2 * LANES)], preferred_element_type=F32)
        total = mixed[pair].reshape(rows, width) + total
        hid = resident_feat[pair].reshape(rows, width).astype(F32) + jnp.maximum(total, 0.0)
        hid = hid.astype(BF16)
        hidden[pair] = hid.reshape(2, tile, width)
        hid = hid.astype(F32)
        mean = jnp.mean(hid, axis=-1, keepdims=True)
        centred = hid - mean
        variance = jnp.mean(centred * centred, axis=-1, keepdims=True)
        normed = (centred * lax.rsqrt(variance + 1e-05) * gain[...]).astype(BF16)
        for i, to in enumerate((query, key, value)):
            product = jnp.dot(normed, wqkv[i], preferred_element_type=F32)
            to[pair] = product.reshape(2, tile, width)

    def column(u):
        return pl.ds(u * LANES, LANES)

    def score_rows(i, carry):
        at = pl.ds(pl.multiple_of(i * 16, 16), 16)
        for t in range(snaps):
            for u in range(t + 1):
                total = query[t, at, column(0)] * key[u, at, column(0)]
                for v in range(1, chunks):
                    total = total + query[t, at, column(v)] * key[u, at, column(v)]
                partial[t, at, column(u)] = total.astype(BF16)
        return carry

    lax.fori_loop(0, tile // 32, lambda i, x: score_rows(2 * i + 1, score_rows(2 * i, x)), 0)

    for u in range(0, snaps, 2):
        at = pl.ds(u * LANES, 2 * LANES)
        later = (snaps - u) * tile
        summed = jnp.dot(
            partial[u:, :, at].reshape(later, 2 * LANES), head_sum[...], preferred_element_type=F32
        )
        scores[u:, :, at] = summed.reshape(snaps - u, tile, 2 * LANES)

    def context_rows(i, carry):
        at = pl.ds(pl.multiple_of(i * 16, 16), 16)
        for t in range(snaps):
            row = [scores[t, at, column(u)] for u in range(t + 1)]
            top = row[0]
            for x in row[1:]:
                top = jnp.maximum(top, x)
            row = [jnp.exp(x - top) for x in row]
            total = row[0]
            for x in row[1:]:
                total = total + x
            scale = 1.0 / total
            row = [x * scale for x in row]
            for v in range(chunks):
                total = row[0] * value[0, at, column(v)]
                for u in range(1, t + 1):
                    total = total + row[u] * value[u, at, column(v)]
                context[t, at, column(v)] = total.astype(BF16)
        return carry

    lax.fori_loop(0, tile // 32, lambda i, x: context_rows(2 * i + 1, context_rows(2 * i, x)), 0)

    half = snaps // 2
    rows = half * tile
    for h in range(2):
        part_of = pl.ds(h * half, half)
        projected = jnp.dot(context[part_of].reshape(rows, width), wo[...], preferred_element_type=F32)
        result = hidden[part_of].astype(F32) + projected.reshape(half, tile, width)
        out[part_of] = result.astype(BF16)

    for c in range(3, sent):
        relay_sent(c)
        agg_sent(c)


def local_layer(
    snaps,
    ring,
    features,
    tile_rows,
    tile_cols,
    tile_values,
    tile_count,
    w_graph,
    norm_gain,
    w_query,
    w_key,
    w_value,
    w_out,
):
    nodes_dev, width = features.shape[1:]
    slots, tile = tile_values.shape[1:3]
    blocks = nodes_dev // tile
    chunks = width // LANES
    smem = pl.BlockSpec(memory_space=pltpu.SMEM)
    hbm = pl.BlockSpec(memory_space=pltpu.HBM)
    dma = pltpu.SemaphoreType.DMA

    def kernel(*refs):
        layer_kernel(snaps, ring, *refs)

    return pl.pallas_call(
        kernel,
        out_shape=pltpu.VMEM((snaps, tile, width), BF16),
        in_specs=[smem] * 3 + [hbm] * 8,
        out_specs=pl.BlockSpec(memory_space=pltpu.VMEM),
        scratch_shapes=[
            *[pltpu.VMEM((5 * blocks, tile, LANES), BF16)] * (chunks - 1),
            *[pltpu.VMEM((5 * blocks, tile // 2, LANES), BF16)] * 2,
            pltpu.VMEM((blocks, tile, LANES), BF16),
            pltpu.VMEM((slots, tile, tile), BF16),
            pltpu.VMEM((slots + 1, tile, LANES), F32),
            pltpu.VMEM((chunks - 1, blocks, tile, LANES), BF16),
            pltpu.VMEM((chunks - 1, snaps, tile, LANES), BF16),
            pltpu.VMEM((2, blocks, tile // 2, LANES), BF16),
            pltpu.VMEM((2, snaps, tile // 2, LANES), BF16),
            pltpu.VMEM((snaps, tile, width), BF16),
            pltpu.VMEM((snaps, tile, width), F32),
            pltpu.VMEM((snaps, tile, width), BF16),
            pltpu.VMEM((snaps, tile, width), F32),
            pltpu.VMEM((snaps, tile, width), F32),
            pltpu.VMEM((snaps, tile, width), F32),
            pltpu.VMEM((width, width), BF16),
            pltpu.VMEM((1, width), F32),
            pltpu.VMEM((3, width, width), BF16),
            pltpu.VMEM((width, width), BF16),
            pltpu.VMEM((2 * LANES, 2 * LANES), BF16),
            pltpu.VMEM((snaps, tile, snaps * LANES), BF16),
            pltpu.VMEM((snaps, tile, snaps * LANES), F32),
            pltpu.VMEM((snaps, tile, width), BF16),
            *[pltpu.SMEM((slots,), jnp.int32)] * 4,
            pltpu.SMEM((slots,), F32),
            pltpu.SMEM((blocks,), jnp.int32),
            dma((2, chunks + 1)),
            dma((2, chunks + 1)),
            dma((2, chunks + 1)),
            dma((2, chunks + 1)),
            dma((snaps,)),
            dma((snaps,)),
            dma((chunks + 1, snaps)),
            dma((chunks + 1, snaps)),
            dma((8 + chunks,)),
        ],
        compiler_params=pltpu.CompilerParams(
            collective_id=0, has_side_effects=True, vmem_limit_bytes=58 * 2**20
        ),
        cost_estimate=pl.CostEstimate(
            flops=4 * 10**9, bytes_accessed=6 * 2**20, transcendentals=10**6
        ),
    )(
        tile_rows,
        tile_cols,
        tile_count,
        features.reshape(blocks, tile, width),
        tile_values[0],
        w_graph,
        norm_gain.reshape(1, width),
        w_query,
        w_key,
        w_value,
        w_out,
    )


def solution(mesh):
    snaps, ring = mesh.shape["snap"], mesh.shape["node"]

    def local(*args):
        return local_layer(snaps, ring, *args)

    in_specs = (
        P("snap", "node", None),
        P("snap", "node"),
        P("snap", "node"),
        P("snap", "node", None, None),
        P("snap", "node"),
        P(),
        P(),
        P(),
        P(),
        P(),
        P(),
    )
    return jax.shard_map(
        local, mesh=mesh, in_specs=in_specs, out_specs=P(None, ("node", "snap"), None), check_vma=False
    )
```
